32 devices in a mesh: rep: 8 (over y, x, core), tp: 4 (over z).
Axes of the slice: x: 2, y: 2, z: 4, core: 2. Of those that a mesh axis runs over, the one named last changes fastest.
Arguments:
- queries: bfloat16 [8, 4, 16384], P('rep'), may hold values from -18 to 18
- cache_keys: bfloat16 [8, 4, 16, 64, 256], P('rep', 'tp'), may hold values from -8 to 8
- cache_values: bfloat16 [8, 4, 16, 64, 256], P('rep', 'tp'), may hold values from -6 to 6
- page_table: int32 [8, 4, 16], P('rep', 'tp'), may hold values from 0 to 15, each once within a row
- lengths: int32 [8], P('rep'), may hold values from 4 to 1024, as said below
- history: bfloat16 [8, 12, 16384], P('rep', None, 'tp'), may hold values from -10 to 10
- norm_gain: float32 [16384], P('tp'), may hold values from 0.5 to 2
- draft_weight: float32 [16384, 16384], P('tp', 'rep'), may hold values from -0.1640625 to 0.1640625
- targets: int32 [8, 16], replicated, may hold values from 0 to 16383
- accepted: int32 [8], replicated, may hold values from 1 to 16, as said below
Outputs:
- attended: bfloat16 [8, 4, 16384], P('rep', None, 'tp')
- new_weight: float32 [16384, 16384], P('tp', 'rep')
The draws below stay inside these ranges and needn't reach their ends.
Inputs may be any that keep to these rules, and one draw needn't show every extreme that they name: `lengths`: some replica's sequence has length exactly 1024. `accepted`: some replica trains all 16 rows.
All inputs are finite; a program needn't handle non-finite values.
Results may differ from the reference program's by a relative error of at most 0.01.
Values may be sent and summed in bfloat16 or wider, within the bound.
No kernel may reach another device: no remote copies, remote signals or barrier semaphores. Data moves between devices by JAX's collectives and lax.ppermute only.
A program may use at most 128 MiB of HBM per device.

```python
import math
import jax
import jax.numpy as jnp
from jax import lax

HQ = 128
KVH = 8
HD = 128
D = 16384
VOCAB = 16384
STEPS = 4
PAGE = 64
MAXP = 16
HIST = 12
ROWS = 16
KVD = 2
CP = 1
MAXLEN = 1024
N_REP = 8
N_TP = 4


def draw_queries(key, part):
    base = jax.random.truncated_normal(jax.random.fold_in(key, 11), -6.0, 6.0, (N_REP, STEPS, D), jnp.float32)
    return base.astype(jnp.bfloat16)


def draw_cache_keys(key, part):
    base = jax.random.truncated_normal(jax.random.fold_in(key, 21), -6.0, 6.0, (N_REP, N_TP, MAXP, PAGE, KVD * HD), jnp.float32)
    return base.astype(jnp.bfloat16)


def draw_history(key, part):
    shape = (N_REP, HIST, D)
    base = jax.random.truncated_normal(jax.random.fold_in(key, 31), -6.0, 6.0, shape, jnp.float32)
    return base.astype(jnp.bfloat16)


def draw_draft_weight(key, part):
    base = 3.0 * jax.random.truncated_normal(jax.random.fold_in(key, 41), -6.0, 6.0, (D, VOCAB), jnp.float32) * D ** (-0.5)
    return base


def draw_lengths(key, part):
    first, second = jax.random.split(key)
    values = jax.random.randint(first, (N_REP,), STEPS, MAXLEN + 1, dtype=jnp.int32)
    chosen = jax.random.randint(second, (), 0, N_REP, dtype=jnp.int32)
    return values.at[chosen].set(MAXLEN)


def draw_accepted(key, part):
    first, second = jax.random.split(jax.random.fold_in(key, 7))
    values = jax.random.randint(first, (N_REP,), 1, ROWS + 1, dtype=jnp.int32)
    chosen = jax.random.randint(second, (), 0, N_REP, dtype=jnp.int32)
    return values.at[chosen].set(ROWS)


def touch_ends(entries, stream_key, least, top_value):
    longest = entries.shape.index(max(entries.shape))
    spots = []
    for shift in (0, 1):
        where = [jax.random.randint(jax.random.fold_in(stream_key, axis), (), 0, length) for axis, length in enumerate(entries.shape)]
        where[longest] = (where[longest] + shift) % entries.shape[longest]
        spots.append(tuple(where))
    return entries.at[spots[0]].set(least).at[spots[1]].set(top_value)


def level_of(rng, shape, shards, low, top_value):
    def one(dim, shards_of):
        heights = jax.random.uniform(jax.random.fold_in(jax.random.fold_in(rng, 6), dim), (shards_of,), jnp.float32, low / len(shards), top_value / len(shards))
        return jnp.repeat(jnp.exp(heights), shape[dim] // shards_of).reshape((-1,) + (1,) * (len(shape) - dim - 1))

    gain = one(*shards[0])
    for cut in shards[1:]:
        gain = gain * one(*cut)
    return gain


def gaussian(own_key, extent, width, most, pieces=(), kind=jnp.bfloat16):
    array = jax.random.normal(own_key, extent, jnp.float32) * width
    if len(pieces) > 0:
        array = level_of(own_key, extent, pieces, -0.22, 0.18) * array
    return jnp.clip(array, min=-most, max=most).astype(kind)


def setup_inputs(seed: int = 0) -> dict:
    key_list = jax.random.split(jax.random.key(seed), 11)
    queries = draw_queries(jax.random.fold_in(key_list[10], 71), 0)
    cache_keys = draw_cache_keys(jax.random.fold_in(key_list[10], 71), 0)
    cache_values = gaussian(key_list[2], (N_REP, N_TP, MAXP, PAGE, KVD * HD), 1.0, 6.0, ((0, 8), (1, 4)))
    page_table = jax.vmap(lambda own: jax.random.permutation(own, MAXP))(jax.random.split(key_list[3], N_REP * N_TP)).reshape((N_REP, N_TP, MAXP)).astype(jnp.int32)
    lengths = draw_lengths(jax.random.fold_in(key_list[10], 71), 0)
    history = draw_history(jax.random.fold_in(key_list[10], 71), 0)
    norm_gain = jnp.clip(jnp.exp(math.log(2.0) - 1.3862944 * jax.random.uniform(key_list[6], (D,), jnp.float32) ** level_of(key_list[6], (D,), ((0, 4),), -0.2, 0.2)), 0.5, 2.0)
    draft_weight = draw_draft_weight(jax.random.fold_in(key_list[10], 71), 0)
    targets = touch_ends(jax.random.randint(key_list[8], (N_REP, ROWS), 0, VOCAB), jax.random.fold_in(key_list[8], 1), 0, VOCAB - 1).astype(jnp.int32)
    accepted = draw_accepted(jax.random.fold_in(key_list[10], 71), 0)
    return {"queries": queries, "cache_keys": cache_keys, "cache_values": cache_values, "page_table": page_table, "lengths": lengths, "history": history, "norm_gain": norm_gain, "draft_weight": draft_weight, "targets": targets, "accepted": accepted}


learn_rate = 0.5

def one_replica(items):
    query, key_pages, value_pages, table, length = items
    groups = N_TP // CP
    owners = jnp.arange(N_TP, dtype=jnp.int32)[:, None]

    def arrange(pages):
        picked = pages[owners, table].reshape(groups, CP, MAXP, PAGE, KVD, HD)
        return picked.transpose(0, 4, 2, 1, 3, 5).reshape(KVH, MAXLEN, HD)
    keys = arrange(key_pages).astype(jnp.float32)
    values = arrange(value_pages).astype(jnp.float32)
    position = jnp.arange(MAXLEN, dtype=jnp.int32)
    limit = length - STEPS + jnp.arange(STEPS, dtype=jnp.int32)
    valid = (position[None, :] <= limit[:, None])[:, None, None, :]
    grouped = query.astype(jnp.float32).reshape(STEPS, KVH, HQ // KVH, HD)
    scores = jnp.einsum('skgd,kpd->skgp', grouped, keys) * HD ** (-0.5)
    top = lax.optimization_barrier(jnp.max(jnp.where(valid, scores, -1e+30), axis=-1))
    expo = jnp.where(valid, jnp.exp(scores - top[..., None]), 0.0)
    total = lax.optimization_barrier(jnp.sum(expo, axis=-1))
    weighted = jnp.einsum('skgp,kpd->skgd', expo, values)
    return (weighted / total[..., None]).reshape(STEPS, D).astype(jnp.bfloat16)

def reference(queries, cache_keys, cache_values, page_table, lengths, history, norm_gain, draft_weight, targets, accepted):
    attended = lax.map(one_replica, (queries, cache_keys, cache_values, page_table, lengths))
    raw = jnp.concatenate([attended, history], axis=1)
    wide = raw.astype(jnp.float32)
    normed = wide * lax.rsqrt(lax.optimization_barrier(jnp.mean(wide * wide, axis=-1, keepdims=True)) + 1e-05) * norm_gain
    rows = normed.reshape(N_REP * ROWS, D)
    logits = jnp.dot(rows, draft_weight, precision=lax.Precision.HIGHEST, preferred_element_type=jnp.float32)
    top = lax.optimization_barrier(jnp.max(logits, axis=-1, keepdims=True))
    expo = jnp.exp(logits - top)
    probs = expo / lax.optimization_barrier(jnp.sum(expo, axis=-1, keepdims=True))
    onehot = (targets.reshape(-1)[:, None] == jnp.arange(VOCAB, dtype=jnp.int32)[None, :]).astype(jnp.float32)
    keep = (jnp.arange(ROWS, dtype=jnp.int32)[None, :] < accepted[:, None]).reshape(-1).astype(jnp.float32)
    delta = (probs - onehot) * keep[:, None]
    grad = jnp.dot(rows.T, delta, precision=lax.Precision.HIGHEST, preferred_element_type=jnp.float32)
    return (attended, draft_weight - learn_rate * grad)
```

```python
import functools

import jax
import jax.numpy as jnp
from jax import lax
from jax.experimental import pallas as pl
from jax.experimental.pallas import tpu as pltpu
from jax.sharding import PartitionSpec as P

HQ = 128
KVH = 8
HD = 128
D = 16384

learn_rate = 0.5
LANES = 128
MIB = 1024 * 1024
TILE = 512
HEIGHT = 256
HELD = (512, 1024)
AGAIN = (1024, 512)
bf16 = jnp.bfloat16
f32 = jnp.float32


def partner_2(value, axis, distance):
    mask = 2**distance
    pairs = [(source, source ^ mask) for source in range(lax.axis_size(axis))]
    return lax.ppermute(value, axis, pairs)


def merged(value, axis, join):
    pieces = jax.tree.map(lambda part: lax.all_gather(part, axis), value)
    head = jax.tree.map(lambda part: part[0], pieces)
    tail = jax.tree.map(lambda part: part[1:], pieces)
    so_far, _ = lax.scan(lambda so_far, share: (join(so_far, share), None), head, tail)
    return so_far


def attend(query, keys, values, position, length, kv_local, group_heads):
    steps = query.shape[0]
    limit = length - steps + jnp.arange(steps, dtype=jnp.int32)
    valid = (position[None, :] <= limit[:, None])[:, None, None, :]
    grouped = query.astype(f32).reshape(steps, kv_local, group_heads, HD)
    scores = jnp.einsum("skgd,pkd->skgp", grouped, keys.astype(f32)) * HD ** (-0.5)
    top = jnp.max(jnp.where(valid, scores, -1e30), axis=-1)
    expo = jnp.where(valid, jnp.exp(scores - top[..., None]), 0.0)
    total = jnp.sum(expo, axis=-1)
    weighted = jnp.einsum("skgp,pkd->skgd", expo, values.astype(f32))
    return (top, total, weighted)


def join_softmax(first, second):
    top = jnp.maximum(first[0], second[0])
    left = jnp.exp(first[0] - top)
    right = jnp.exp(second[0] - top)
    return (
        top,
        first[1] * left + second[1] * right,
        first[2] * left[..., None] + second[2] * right[..., None],
    )


def join_stats(first, second):
    top = jnp.maximum(first[0], second[0])
    return (top, first[1] * jnp.exp(first[0] - top) + second[1] * jnp.exp(second[0] - top))


def general_plan(
    queries,
    cache_keys,
    cache_values,
    page_table,
    lengths,
    history,
    norm_gain,
    draft_weight,
    targets,
    accepted,
):
    owner = lax.axis_index("tp")
    owners = lax.axis_size("tp")
    kv_local = cache_keys.shape[4] // HD
    sharing = max(1, owners // KVH)
    group_heads = HQ // KVH
    own_heads = HQ // owners
    segment = owner % sharing
    first_head = owner // sharing * kv_local
    table = page_table[0, 0]
    keys = cache_keys[0, 0][table].reshape(-1, kv_local, HD)
    values = cache_values[0, 0][table].reshape(-1, kv_local, HD)
    pages = table.shape[0]
    slots = cache_keys.shape[3]
    position = (
        (jnp.arange(pages, dtype=jnp.int32)[:, None] * sharing + segment) * slots
        + jnp.arange(slots, dtype=jnp.int32)[None, :]
    ).reshape(-1)
    span = kv_local * group_heads * HD
    query = lax.dynamic_slice_in_dim(queries[0], first_head * group_heads * HD, span, 1)
    state = attend(query, keys, values, position, lengths[0], kv_local, group_heads)
    for section in range(sharing.bit_length() - 1):
        partner = partner_2((state[0], state[1], state[2]), "tp", section)
        state = join_softmax(state, partner)
    top, total, weighted = state
    steps = query.shape[0]
    heads = (weighted / total[..., None]).reshape(steps, kv_local * group_heads, HD)
    chosen = lax.dynamic_slice_in_dim(heads, segment * own_heads, own_heads, 1)
    attended = chosen.reshape(1, steps, own_heads * HD).astype(bf16)
    raw = jnp.concatenate([attended[0], history[0]], axis=0)
    rows_each = raw.shape[0]
    wide = raw.astype(f32)
    squares = lax.psum(jnp.sum(wide * wide, axis=-1), "tp")
    row_scale = lax.rsqrt(squares / D + 1e-05)
    scaled_rows = wide * row_scale[:, None] * norm_gain
    gathered = lax.all_gather(scaled_rows, "rep", axis=0, tiled=True)
    partial_value = jnp.dot(
        gathered, draft_weight, precision=lax.Precision.HIGHEST, preferred_element_type=f32
    )
    logits = lax.psum(partial_value, "tp")
    columns = draft_weight.shape[1]
    column_start = lax.axis_index("rep") * columns
    local_top = jnp.max(logits, axis=-1)
    local_total = jnp.sum(jnp.exp(logits - local_top[:, None]), axis=-1)
    top_all, total_all = merged((local_top, local_total), "rep", join_stats)
    probs = jnp.exp(logits - top_all[:, None]) / total_all[:, None]
    labels = column_start + jnp.arange(columns, dtype=jnp.int32)
    onehot = (targets.reshape(-1)[:, None] == labels[None, :]).astype(f32)
    keep = (
        (jnp.arange(rows_each, dtype=jnp.int32)[None, :] < accepted[:, None])
        .reshape(-1)
        .astype(f32)
    )
    delta = (probs - onehot) * keep[:, None]
    grad = jnp.dot(gathered.T, delta, precision=lax.Precision.HIGHEST, preferred_element_type=f32)
    return (attended, draft_weight - learn_rate * grad)


def exchange(value, axis, mask):
    pairs = [(source, source ^ mask) for source in range(lax.axis_size(axis))]
    return lax.ppermute(value, axis, pairs)


def whole(space=pltpu.VMEM):
    return pl.BlockSpec(memory_space=space)


def in_hbm(value):
    return pltpu.with_memory_space_constraint(value, pltpu.HBM)


def attention_kernel(
    kv_local,
    table_ref,
    length_ref,
    queries_ref,
    keys_ref,
    values_ref,
    history_ref,
    weight_ref,
    raw_ref,
    attended_ref,
    held_ref,
    query_buf,
    key_buf,
    value_buf,
    history_buf,
    query_sem,
    key_sem,
    value_sem,
    history_sem,
    weight_sem,
):
    pages, slots = keys_ref.shape[0], keys_ref.shape[1]
    steps = query_buf.shape[0]
    group = HQ // KVH
    span = query_buf.shape[1]
    start = pl.multiple_of(lax.axis_index("tp") * span, span)
    query_copy = pltpu.make_async_copy(queries_ref.at[:, pl.ds(start, span)], query_buf, query_sem)
    query_copy.start()
    key_copies, value_copies = [], []
    for source, target, sems, copies in (
        (keys_ref, key_buf, key_sem, key_copies),
        (values_ref, value_buf, value_sem, value_copies),
    ):
        for page in range(pages):
            copy = pltpu.make_async_copy(
                source.at[table_ref[page]], target.at[pl.ds(page * slots, slots)], sems.at[page]
            )
            copy.start()
            copies.append(copy)
    history_copy = pltpu.make_async_copy(history_ref, history_buf, history_sem)
    history_copy.start()
    query_copy.wait()
    queries = query_buf[...].astype(f32)
    stacked = []
    for head in range(kv_local):
        parts = [
            queries[:, (head * group + g) * HD : (head * group + g + 1) * HD] for g in range(group)
        ]
        stacked.append(jnp.concatenate(parts, axis=0).astype(bf16))
    for copy in key_copies + value_copies:
        copy.wait()
    weight_copies = column_copies(weight_ref, held_ref, weight_sem, 0)
    for copy in weight_copies:
        copy.start()
    shape = (group * steps, pages * slots)
    step = lax.broadcasted_iota(jnp.int32, shape, 0) % steps
    position = lax.broadcasted_iota(jnp.int32, shape, 1)
    valid = position <= length_ref[0] - steps + step
    expos, totals = [], []
    for head in range(kv_local):
        scores = lax.dot_general(
            stacked[head],
            key_buf[:, head * HD : (head + 1) * HD],
            (((1,), (1,)), ((), ())),
            preferred_element_type=f32,
        ) * (HD ** (-0.5))
        top = jnp.max(jnp.where(valid, scores, -1e30), axis=-1, keepdims=True)
        expo = jnp.where(valid, jnp.exp(scores - top), 0.0)
        totals.append(jnp.sum(expo, axis=-1, keepdims=True))
        expos.append(jnp.concatenate(split2(expo), axis=0))
    history_copy.wait()
    for head in range(kv_local):
        both = jnp.dot(
            expos[head],
            value_buf[:, head * HD : (head + 1) * HD],
            preferred_element_type=f32,
        )
        half = group * steps
        out = (both[:half] + both[half:]) / totals[head]
        for g in range(group):
            columns = slice((head * group + g) * HD, (head * group + g + 1) * HD)
            piece = out[g * steps : (g + 1) * steps]
            earlier = history_buf[:, columns].astype(f32)
            raw_ref[:, columns] = jnp.concatenate([piece, earlier], axis=0).astype(bf16)
            attended_ref[:, columns] = piece.astype(bf16)
    for copy in weight_copies:
        copy.wait()


def run_attention(queries, keys, values, table, length, history, weight, held):
    pages, slots, width = keys.shape
    kv_local = width // HD
    steps = queries.shape[0]
    span = kv_local * (HQ // KVH) * HD
    rows = steps + history.shape[0]
    return pl.pallas_call(
        functools.partial(attention_kernel, kv_local),
        out_shape=(
            jax.ShapeDtypeStruct((rows, span), bf16),
            jax.ShapeDtypeStruct((steps, span), bf16),
            pltpu.VMEM((weight.shape[0], held), f32),
        ),
        in_specs=[
            whole(pltpu.SMEM),
            whole(pltpu.SMEM),
            whole(pltpu.HBM),
            whole(pltpu.HBM),
            whole(pltpu.HBM),
            whole(pltpu.HBM),
            whole(pltpu.HBM),
        ],
        out_specs=(whole(), whole(), whole()),
        scratch_shapes=[
            pltpu.VMEM((steps, span), bf16),
            pltpu.VMEM((pages * slots, width), bf16),
            pltpu.VMEM((pages * slots, width), bf16),
            pltpu.VMEM(history.shape, bf16),
            pltpu.SemaphoreType.DMA,
            pltpu.SemaphoreType.DMA((pages,)),
            pltpu.SemaphoreType.DMA((pages,)),
            pltpu.SemaphoreType.DMA,
            pltpu.SemaphoreType.DMA((held // 256,)),
        ],
        compiler_params=pltpu.CompilerParams(vmem_limit_bytes=12 * MIB),
        cost_estimate=pl.CostEstimate(
            flops=4 * 64 * 1024 * 256, bytes_accessed=12 * MIB, transcendentals=131072
        ),
        name="attention",
    )(table, length, *(in_hbm(part) for part in (queries, keys, values, history, weight)))


def column_copies(source, target, sems, first, width=256):
    return [
        pltpu.make_async_copy(
            source.at[:, pl.ds(first + place, width)],
            target.at[:, pl.ds(place, width)],
            sems.at[index],
        )
        for index, place in enumerate(range(0, target.shape[1], width))
    ]


def load_kernel(first, count, weight_ref, token_ref, *refs):
    held_refs, done_ref, sems = refs[:count], refs[count], refs[count + 1]
    done_ref[...] = jnp.zeros(done_ref.shape, f32)
    copies = []
    for ref in held_refs:
        tiles = len(copies)
        copies += column_copies(weight_ref, ref, sems.at[pl.ds(tiles, ref.shape[1] // 256)], first)
        first += ref.shape[1]
    for copy in copies:
        copy.start()
    for copy in copies:
        copy.wait()


def run_load(weight, token, first, widths):
    rows = weight.shape[0]
    columns = sum(widths)
    *helds, done = pl.pallas_call(
        functools.partial(load_kernel, first, len(widths)),
        out_shape=tuple(pltpu.VMEM((rows, width), f32) for width in widths)
        + (jax.ShapeDtypeStruct((8, LANES), f32),),
        in_specs=[whole(pltpu.HBM), whole(pl.ANY)],
        out_specs=tuple(whole() for _ in range(len(widths) + 1)),
        scratch_shapes=[pltpu.SemaphoreType.DMA((columns // 256,))],
        compiler_params=pltpu.CompilerParams(vmem_limit_bytes=8 * MIB),
        cost_estimate=pl.CostEstimate(
            flops=0, bytes_accessed=4 * rows * columns, transcendentals=0
        ),
        name="load_weight",
    )(in_hbm(weight), token)
    return [pltpu.with_memory_space_constraint(held, pltpu.VMEM) for held in helds], done


def split2(value):
    high = value.astype(bf16)
    return high, (value - high.astype(f32)).astype(bf16)


def stack_kernel(*refs):
    each = refs[0].shape[0]
    for k, ref in enumerate(refs[:-2]):
        refs[-1][k * each : (k + 1) * each, :] = ref[...]


def run_stack(parts, after):
    each, features = parts[0].shape
    return pl.pallas_call(
        stack_kernel,
        out_shape=jax.ShapeDtypeStruct((len(parts) * each, features), bf16),
        in_specs=[whole() for _ in parts] + [whole(pl.ANY)],
        out_specs=whole(),
        compiler_params=pltpu.CompilerParams(vmem_limit_bytes=4 * MIB),
        cost_estimate=pl.CostEstimate(flops=4096, bytes_accessed=4096, transcendentals=0),
        name="stacked_rows",
    )(*parts, after)


def power_above(value):
    exponent = jnp.full(value.shape, -96.0, f32)
    for step in (128.0, 64.0, 32.0, 16.0, 8.0, 4.0, 2.0, 1.0):
        exponent = jnp.where(value > jnp.exp2(exponent + (step - 1.0)), exponent + step, exponent)
    return exponent


def logits_kernel(n_rep, n_tp, *refs):
    block_refs = refs[:2]
    gain_ref, *held_refs, weight_ref = refs[2:6]
    x_ref, own_ref, square_ref = refs[6:9]
    send_refs = refs[9 : 8 + n_tp]
    scaled_buf, partial_buf, rest_buf, rest_sem = refs[8 + n_tp :]
    tile = pl.program_id(0)
    rep, tp = lax.axis_index("rep"), lax.axis_index("tp")
    rows = x_ref.shape[0]
    each = rows // n_rep
    share = rows // n_tp
    width = partial_buf.shape[1] // pl.num_programs(0)
    held_columns = sum(ref.shape[1] for ref in held_refs)
    copies = column_copies(weight_ref, rest_buf, rest_sem, held_columns, width)

    @pl.when(tile == 0)
    def _():
        for copy in copies:
            copy.start()
        for k in range(n_rep):
            block = block_refs[k % 2][k // 2 * each : (k // 2 + 1) * each, :]
            place = pl.multiple_of(lax.bitwise_xor(rep, k) * each, each)
            x_ref[pl.ds(place, each), :] = block
            value = block.astype(f32)
            squares = jnp.sum(value * value, axis=-1, keepdims=True)
            square_ref[pl.ds(place, each), :] = jnp.broadcast_to(squares, (each, LANES))
            scaled_buf[pl.ds(place, each), :] = (value * gain_ref[...]).astype(bf16)

    columns = pl.ds(pl.multiple_of(tile * width, width), width)

    def multiply(weight):
        partial_buf[:, columns] = jnp.dot(
            scaled_buf[...], weight.astype(bf16), preferred_element_type=f32
        )

    first = 0
    for ref in held_refs:
        for index in range(ref.shape[1] // width):

            @pl.when(tile == first + index)
            def _():
                multiply(ref[:, index * width : (index + 1) * width])

        first += ref.shape[1] // width
    for index, copy in enumerate(copies):

        @pl.when(tile == first + index)
        def _():
            copy.wait()
            multiply(rest_buf[:, index * width : (index + 1) * width])

    @pl.when(tile == pl.num_programs(0) - 1)
    def _():
        own_ref[...] = partial_buf[pl.ds(pl.multiple_of(tp * share, share), share), :]
        full = partial_buf.shape[1]
        lane = lax.broadcasted_iota(jnp.int32, (share, LANES), 1)
        squares = jnp.zeros((share, LANES), f32)
        group = LANES // n_tp
        for j in range(n_tp):
            mine = (lane >= j * group) & (lane < (j + 1) * group)
            squares = jnp.where(mine, square_ref[j * share : (j + 1) * share, :], squares)
        first = jnp.floor(squares / 16.0)
        second = jnp.floor((squares - first * 16.0) * 2048.0)
        third = jnp.floor((squares - first * 16.0 - second / 2048.0) * 2.0**26)
        part = lane % group
        extra = jnp.where(part == 0, first, jnp.where(part == 1, second, third))
        for k in range(1, n_tp):
            place = pl.multiple_of(lax.bitwise_xor(tp, k) * share, share)
            value = partial_buf[pl.ds(place, share), :]
            exponent = power_above(jnp.max(jnp.abs(value), axis=-1, keepdims=True))
            coded = jnp.floor(value * jnp.exp2(15.0 - exponent) + 0.5)
            coded = jnp.clip(coded, -32768.0, 32767.0)
            send_refs[k - 1][:, :full] = coded.astype(jnp.int32).astype(jnp.int16)
            tail = jnp.where(part == 3, exponent, extra)
            send_refs[k - 1][:, full:] = tail.astype(jnp.int32).astype(jnp.int16)


def run_logits(blocks, gain, helds, weight, n_rep, n_tp):
    rows, features = 2 * blocks[0].shape[0], blocks[0].shape[1]
    columns = weight.shape[1]
    share = rows // n_tp
    tiles = columns // TILE
    rest = columns - sum(held.shape[1] for held in helds)
    return pl.pallas_call(
        functools.partial(logits_kernel, n_rep, n_tp),
        grid=(tiles,),
        out_shape=(
            jax.ShapeDtypeStruct((rows, features), bf16),
            jax.ShapeDtypeStruct((share, columns), f32),
            jax.ShapeDtypeStruct((rows, LANES), f32),
        )
        + tuple(
            jax.ShapeDtypeStruct((share, columns + LANES), jnp.int16) for _ in range(n_tp - 1)
        ),
        in_specs=[whole() for _ in range(3 + len(helds))] + [whole(pltpu.HBM)],
        out_specs=tuple(whole() for _ in range(n_tp + 2)),
        scratch_shapes=[
            pltpu.VMEM((rows, features), bf16),
            pltpu.VMEM((rows, columns), f32),
            pltpu.VMEM((features, rest), f32),
            pltpu.SemaphoreType.DMA((rest // TILE,)),
        ],
        compiler_params=pltpu.CompilerParams(vmem_limit_bytes=14 * MIB),
        cost_estimate=pl.CostEstimate(
            flops=6 * rows * features * columns,
            bytes_accessed=4 * features * columns,
            transcendentals=0,
        ),
        name="partial_logits",
    )(*blocks, gain, *helds, in_hbm(weight))


def decoded(ref, columns):
    share = ref.shape[0]
    tail = ref[:, columns:].astype(jnp.int32).astype(f32)
    part = lax.broadcasted_iota(jnp.int32, (share, LANES), 1) % (LANES // lax.axis_size("tp"))
    unit = jnp.where(part == 0, 16.0, jnp.where(part == 1, 1.0 / 2048.0, 2.0**-26))
    unit = jnp.where(part < 3, unit, 0.0)
    value = ref[:, :columns].astype(jnp.int32).astype(f32)
    return value * jnp.exp2(tail[:, 3:4] - 15.0), tail * unit


def first_sum_kernel(own_ref, received_ref, sum_ref, square_ref):
    value, squares = decoded(received_ref, own_ref.shape[1])
    sum_ref[...] = own_ref[...] + value
    square_ref[...] = squares


def run_first_sum(own, received):
    share, columns = own.shape
    return pl.pallas_call(
        first_sum_kernel,
        out_shape=(
            jax.ShapeDtypeStruct((share, columns), f32),
            jax.ShapeDtypeStruct((share, LANES), f32),
        ),
        in_specs=[whole(), whole()],
        out_specs=(whole(), whole()),
        compiler_params=pltpu.CompilerParams(vmem_limit_bytes=8 * MIB),
        cost_estimate=pl.CostEstimate(flops=65536, bytes_accessed=65536, transcendentals=0),
        name="first_sum",
    )(own, received)


def softmax_kernel(n_tp, n_more, sum_ref, square_ref, first_ref, *refs):
    received = refs[: n_tp - 2]
    expo_ref, scale_ref = refs[n_tp - 2 + n_more : n_tp + n_more]
    share, columns = sum_ref.shape
    group = LANES // n_tp
    lane = lax.broadcasted_iota(jnp.int32, (share, LANES), 1)
    logits, squares = sum_ref[...], first_ref[...]
    for ref in received:
        value, more = decoded(ref, columns)
        logits, squares = logits + value, squares + more
    for j in range(n_tp):
        rows = slice(j * share, (j + 1) * share)
        mine = jnp.where((lane >= j * group) & (lane < (j + 1) * group), squares, 0.0)
        total = square_ref[rows, :] + jnp.sum(mine, axis=-1, keepdims=True)
        scale_ref[rows, :] = lax.rsqrt(total / D + 1e-05)
    tp = lax.axis_index("tp")
    scale = scale_ref[pl.ds(pl.multiple_of(tp * share, share), share), :]
    logits = logits * scale[:, :1]
    top = jnp.max(logits, axis=-1, keepdims=True)
    expo = jnp.exp(logits - top)
    total = jnp.sum(expo, axis=-1, keepdims=True)
    expo_ref[:, :columns] = expo.astype(bf16)
    for first, value in ((0, top), (3, total)):
        for place in range(first, first + 3):
            high = value.astype(bf16)
            expo_ref[:, columns + place : columns + place + 1] = high
            value = value - high.astype(f32)


def held_shapes(helds):
    return tuple(pltpu.VMEM(held.shape, f32) for held in helds)


def run_softmax(partly, squares, first, received, after, helds):
    share, columns = partly.shape
    rows = squares.shape[0]
    return pl.pallas_call(
        functools.partial(softmax_kernel, len(received) + 2, len(after) + len(helds)),
        out_shape=(
            jax.ShapeDtypeStruct((share, columns + LANES), bf16),
            jax.ShapeDtypeStruct((rows, LANES), f32),
        )
        + held_shapes(helds),
        in_specs=[whole() for _ in range(len(received) + 3)] + [whole(pl.ANY) for _ in after]
        + [whole() for _ in helds],
        out_specs=tuple(whole() for _ in range(2 + len(helds))),
        input_output_aliases={len(received) + len(after) + 3 + i: 2 + i for i in range(len(helds))},
        compiler_params=pltpu.CompilerParams(vmem_limit_bytes=8 * MIB),
        cost_estimate=pl.CostEstimate(flops=65536, bytes_accessed=65536, transcendentals=0),
        name="local_softmax",
    )(partly, squares, first, *received, *after, *helds)


def stats_kernel(n_tp, n_held, *refs):
    stats, out_ref, column_buf = refs[:n_tp], refs[n_tp + n_held], refs[-1]
    share = stats[0].shape[0]
    tp = lax.axis_index("tp")
    lane = lax.broadcasted_iota(jnp.int32, (share, LANES), 1)
    for k, ref in enumerate(stats):
        parts = ref[:, ref.shape[1] - LANES :].astype(f32)
        top = parts[:, 0:1] + parts[:, 1:2] + parts[:, 2:3]
        total = parts[:, 3:4] + parts[:, 4:5] + parts[:, 5:6]
        place = pl.multiple_of(lax.bitwise_xor(tp, k) * share, share)
        column_buf[pl.ds(place, share), :] = jnp.where(lane == 0, top, total)
    out_ref[...] = column_buf[...].T[:8, :]


def run_stats(lefts, helds):
    rows = len(lefts) * lefts[0].shape[0]
    return pl.pallas_call(
        functools.partial(stats_kernel, len(lefts), len(helds)),
        out_shape=(jax.ShapeDtypeStruct((8, rows), f32),) + held_shapes(helds),
        in_specs=[whole() for _ in range(len(lefts) + len(helds))],
        out_specs=tuple(whole() for _ in range(1 + len(helds))),
        input_output_aliases={len(lefts) + i: 1 + i for i in range(len(helds))},
        scratch_shapes=[pltpu.VMEM((rows, LANES), f32)],
        compiler_params=pltpu.CompilerParams(vmem_limit_bytes=8 * MIB),
        cost_estimate=pl.CostEstimate(flops=65536, bytes_accessed=65536, transcendentals=0),
        name="row_stats",
    )(*lefts, *helds)


def joined(stats):
    top = stats[0][0:1, :]
    for ref in stats[1:]:
        top = jnp.maximum(top, ref[0:1, :])
    total = jnp.zeros_like(top)
    for ref in stats:
        total = total + ref[1:2, :] * jnp.exp(ref[0:1, :] - top)
    return top, total


def join_kernel(first_ref, second_ref, out_ref):
    top, total = joined((first_ref, second_ref))
    row = lax.broadcasted_iota(jnp.int32, out_ref.shape, 0)
    out_ref[...] = jnp.where(row == 0, top, total)


def run_join(first, second):
    return pl.pallas_call(
        join_kernel,
        out_shape=jax.ShapeDtypeStruct(first.shape, f32),
        in_specs=[whole(), whole()],
        out_specs=whole(),
        compiler_params=pltpu.CompilerParams(vmem_limit_bytes=4 * MIB),
        cost_estimate=pl.CostEstimate(flops=4096, bytes_accessed=4096, transcendentals=0),
        name="pair_stats",
    )(first, second)


def turn_kernel(x_ref, gain_ref, out_ref):
    out_ref[...] = (x_ref[...].astype(f32) * gain_ref[...]).T


def run_turn(x, gain):
    rows, features = x.shape
    tile = 1024
    return pl.pallas_call(
        turn_kernel,
        grid=(features // tile,),
        out_shape=jax.ShapeDtypeStruct((features, rows), f32),
        in_specs=[
            pl.BlockSpec((rows, tile), lambda i: (0, i)),
            pl.BlockSpec((1, tile), lambda i: (0, i)),
        ],
        out_specs=pl.BlockSpec((tile, rows), lambda i: (i, 0)),
        compiler_params=pltpu.CompilerParams(vmem_limit_bytes=8 * MIB),
        cost_estimate=pl.CostEstimate(flops=4096, bytes_accessed=4096, transcendentals=0),
        name="turned_rows",
    )(x, gain)


def scale_kernel(
    n_held, first, turned_ref, scale_ref, targets_ref, accepted_ref, weight_ref, *refs
):
    out_ref, target_ref = refs[n_held : n_held + 2]
    rest_ref, sems = refs[-2:]
    copies = column_copies(weight_ref, rest_ref, sems, first)
    for copy in copies:
        copy.start()
    rows = turned_ref.shape[1]
    scale = scale_ref[...].T[:1, :] * learn_rate
    high, low = split2(turned_ref[...] * scale)
    out_ref[:, :rows] = high
    out_ref[:, rows:] = low
    each = targets_ref.shape[1]
    row = lax.broadcasted_iota(jnp.int32, (each, LANES), 0)
    for block in range(rows // each):
        target = jnp.zeros((each, LANES), jnp.int32)
        for i in range(each):
            target = jnp.where(row == i, targets_ref[block, i], target)
        target = jnp.where(row < accepted_ref[block], target, -1)
        target_ref[block * each : (block + 1) * each, :] = target
    for copy in copies:
        copy.wait()


def run_scale(turned, scale, targets, accepted, weight, helds):
    features, rows = turned.shape
    first = sum(held.shape[1] for held in helds)
    rest = weight.shape[1] - first
    return pl.pallas_call(
        functools.partial(scale_kernel, len(helds), first),
        out_shape=(
            jax.ShapeDtypeStruct((features, 2 * rows), bf16),
            jax.ShapeDtypeStruct((rows, LANES), jnp.int32),
        )
        + held_shapes(helds)
        + (pltpu.VMEM((features, rest), f32),),
        in_specs=[
            whole(),
            whole(),
            whole(pltpu.SMEM),
            whole(pltpu.SMEM),
            whole(pltpu.HBM),
        ]
        + [whole() for _ in helds],
        out_specs=tuple(whole() for _ in range(3 + len(helds))),
        input_output_aliases={5 + i: 2 + i for i in range(len(helds))},
        scratch_shapes=[pltpu.SemaphoreType.DMA((rest // 256,))],
        compiler_params=pltpu.CompilerParams(vmem_limit_bytes=8 * MIB),
        cost_estimate=pl.CostEstimate(flops=65536, bytes_accessed=65536, transcendentals=0),
        name="scaled_rows",
    )(turned, scale, targets, accepted, in_hbm(weight), *helds)


def update_kernel(n_tp, n_held, *refs):
    turned_ref, target_ref = refs[:2]
    expo_refs = refs[2 : 2 + n_tp]
    n_stats = len(refs) - 2 - n_tp - 2 * n_held - 4
    own_stat_ref, *stat_refs = refs[2 + n_tp : 2 + n_tp + n_stats]
    out_ref, *held_refs = refs[2 + n_tp + n_stats + n_held : -3]
    delta_buf, factor_buf, sems = refs[-3:]
    rep, tp = lax.axis_index("rep"), lax.axis_index("tp")
    share, columns = expo_refs[0].shape[0], expo_refs[0].shape[1] - LANES
    rows = n_tp * share
    top, total = joined(stat_refs)
    factor = jnp.exp(own_stat_ref[0:1, :] - top) / total
    factor = jnp.broadcast_to(factor, (rows, rows)).T
    trained = jnp.where(target_ref[...] >= 0, 1.0, 0.0)
    factor_buf[...] = factor[:, :LANES] * trained
    label = lax.broadcasted_iota(jnp.int32, (share, columns), 1) + rep * columns
    for k in range(n_tp):
        place = pl.multiple_of(lax.bitwise_xor(tp, k) * share, share)
        mine = pl.ds(place, share)
        onehot = jnp.where(label == target_ref[mine, 0:1], 1.0, 0.0)
        delta = expo_refs[k][:, :columns].astype(f32) * factor_buf[mine, 0:1] - onehot
        delta = delta.astype(bf16)
        delta_buf[mine, :] = delta
        delta_buf[pl.ds(pl.multiple_of(rows + place, share), share), :] = delta

    height = HEIGHT
    steps = turned_ref.shape[0] // height

    def copies_of(step):
        mine = pl.ds(pl.multiple_of(step * height, height), height)
        first, copies = 0, []
        for index, ref in enumerate(held_refs):
            target = out_ref.at[mine, pl.ds(first, ref.shape[1])]
            copies.append(pltpu.make_async_copy(ref.at[mine], target, sems.at[index, step]))
            first += ref.shape[1]
        return copies

    def one_step(step, _):
        mine = pl.ds(pl.multiple_of(step * height, height), height)
        grad = jnp.dot(turned_ref[mine, :], delta_buf[...], preferred_element_type=f32)
        first = 0
        for ref in held_refs:
            ref[mine, :] = ref[mine, :] - grad[:, first : first + ref.shape[1]]
            first += ref.shape[1]
        for copy in copies_of(step):
            copy.start()
        return 0

    def one_wait(step, _):
        for copy in copies_of(step):
            copy.wait()
        return 0

    lax.fori_loop(0, steps, one_step, 0)
    lax.fori_loop(0, steps, one_wait, 0)


def run_update(turned, target, expos, stats, helds):
    features, pair = turned.shape
    columns = sum(held.shape[1] for held in helds)
    n_tp, n_held = len(expos), len(helds)
    operands = (turned, target, *expos, *stats, *helds)
    new_weight, *_ = pl.pallas_call(
        functools.partial(update_kernel, n_tp, n_held),
        out_shape=(jax.ShapeDtypeStruct((features, columns), f32),)
        + held_shapes(helds),
        in_specs=[whole() for _ in operands],
        out_specs=(whole(pltpu.HBM),) + tuple(whole() for _ in helds),
        input_output_aliases={len(operands) - n_held + i: 1 + i for i in range(n_held)},
        scratch_shapes=[
            pltpu.VMEM((pair, columns), bf16),
            pltpu.VMEM((pair // 2, LANES), f32),
            pltpu.SemaphoreType.DMA((n_held, features // HEIGHT)),
        ],
        compiler_params=pltpu.CompilerParams(vmem_limit_bytes=10 * MIB),
        cost_estimate=pl.CostEstimate(flops=65536, bytes_accessed=65536, transcendentals=0),
        name="weight_update",
    )(*operands)
    return new_weight


def direct_plan(
    queries,
    cache_keys,
    cache_values,
    page_table,
    lengths,
    history,
    norm_gain,
    draft_weight,
    targets,
    accepted,
):
    n_rep, n_tp = lax.axis_size("rep"), lax.axis_size("tp")
    gain = norm_gain.reshape(1, -1)
    raw, attended, first = run_attention(
        queries[0],
        cache_keys[0, 0],
        cache_values[0, 0],
        page_table[0, 0],
        lengths,
        history[0],
        draft_weight,
        HELD[0],
    )
    first = pltpu.with_memory_space_constraint(first, pltpu.VMEM)
    (second,), loaded = run_load(draft_weight, raw, HELD[0], HELD[1:])
    raws = [raw] + [exchange(raw, "rep", k) for k in range(2, n_rep, 2)]
    block = run_stack(raws, loaded)
    blocks = (block, exchange(block, "rep", 1))
    x, own, squares, *sends = run_logits(
        blocks, gain, (first, second), draft_weight, n_rep, n_tp
    )
    turned = run_turn(x, gain)
    received = [exchange(sends[k - 1], "tp", k) for k in range(1, n_tp)]
    partly, part = run_first_sum(own, received[0])
    helds, loaded = run_load(draft_weight, own, 0, AGAIN)
    expo, scale, *helds = run_softmax(
        partly, squares, part, received[1:], (loaded, turned), helds
    )
    expos = [expo] + [exchange(expo, "tp", k) for k in range(1, n_tp)]
    scaled, target, *helds = run_scale(turned, scale, targets, accepted, draft_weight, helds)
    stat, *helds = run_stats(expos, helds)
    pair = run_join(stat, exchange(stat, "rep", 1))
    stats = [stat, pair] + [exchange(pair, "rep", k) for k in range(2, n_rep, 2)]
    helds = [pltpu.with_memory_space_constraint(held, pltpu.VMEM) for held in helds]
    new_weight = run_update(scaled, target, expos, stats, helds)
    return (attended[None], new_weight)


def solution(mesh):
    plan = direct_plan if (mesh.shape["rep"], mesh.shape["tp"]) == (8, 4) else general_plan
    return jax.shard_map(
        plan,
        mesh=mesh,
        in_specs=(
            P("rep", None, None),
            P("rep", "tp", None, None, None),
            P("rep", "tp", None, None, None),
            P("rep", "tp", None),
            P("rep"),
            P("rep", None, "tp"),
            P("tp"),
            P("tp", "rep"),
            P(),
            P(),
        ),
        out_specs=(P("rep", None, "tp"), P("tp", "rep")),
        check_vma=False,
    )
```

```python
import functools

import jax
import jax.numpy as jnp
from jax import lax
from jax.experimental import pallas as pl
from jax.experimental.pallas import tpu as pltpu
from jax.sharding import PartitionSpec as P

HQ = 128
KVH = 8
HD = 128
D = 16384

learn_rate = 0.5
LANES = 128
MIB = 1024 * 1024
TILE = 512
SUM_ORDER = (2, 1, 3)
BACK_ORDER = (1, 2, 3)
HEIGHT = 256
HELD = (512, 1024)
AGAIN = (768, 1024)
bf16 = jnp.bfloat16
f32 = jnp.float32


def partner_2(value, axis, distance):
    mask = 2**distance
    pairs = [(source, source ^ mask) for source in range(lax.axis_size(axis))]
    return lax.ppermute(value, axis, pairs)


def merged(value, axis, join):
    pieces = jax.tree.map(lambda part: lax.all_gather(part, axis), value)
    head = jax.tree.map(lambda part: part[0], pieces)
    tail = jax.tree.map(lambda part: part[1:], pieces)
    so_far, _ = lax.scan(lambda so_far, share: (join(so_far, share), None), head, tail)
    return so_far


def attend(query, keys, values, position, length, kv_local, group_heads):
    steps = query.shape[0]
    limit = length - steps + jnp.arange(steps, dtype=jnp.int32)
    valid = (position[None, :] <= limit[:, None])[:, None, None, :]
    grouped = query.astype(f32).reshape(steps, kv_local, group_heads, HD)
    scores = jnp.einsum("skgd,pkd->skgp", grouped, keys.astype(f32)) * HD ** (-0.5)
    top = jnp.max(jnp.where(valid, scores, -1e30), axis=-1)
    expo = jnp.where(valid, jnp.exp(scores - top[..., None]), 0.0)
    total = jnp.sum(expo, axis=-1)
    weighted = jnp.einsum("skgp,pkd->skgd", expo, values.astype(f32))
    return (top, total, weighted)


def join_softmax(first, second):
    top = jnp.maximum(first[0], second[0])
    left = jnp.exp(first[0] - top)
    right = jnp.exp(second[0] - top)
    return (
        top,
        first[1] * left + second[1] * right,
        first[2] * left[..., None] + second[2] * right[..., None],
    )


def join_stats(first, second):
    top = jnp.maximum(first[0], second[0])
    return (top, first[1] * jnp.exp(first[0] - top) + second[1] * jnp.exp(second[0] - top))


def general_plan(
    queries,
    cache_keys,
    cache_values,
    page_table,
    lengths,
    history,
    norm_gain,
    draft_weight,
    targets,
    accepted,
):
    owner = lax.axis_index("tp")
    owners = lax.axis_size("tp")
    kv_local = cache_keys.shape[4] // HD
    sharing = max(1, owners // KVH)
    group_heads = HQ // KVH
    own_heads = HQ // owners
    segment = owner % sharing
    first_head = owner // sharing * kv_local
    table = page_table[0, 0]
    keys = cache_keys[0, 0][table].reshape(-1, kv_local, HD)
    values = cache_values[0, 0][table].reshape(-1, kv_local, HD)
    pages = table.shape[0]
    slots = cache_keys.shape[3]
    position = (
        (jnp.arange(pages, dtype=jnp.int32)[:, None] * sharing + segment) * slots
        + jnp.arange(slots, dtype=jnp.int32)[None, :]
    ).reshape(-1)
    span = kv_local * group_heads * HD
    query = lax.dynamic_slice_in_dim(queries[0], first_head * group_heads * HD, span, 1)
    state = attend(query, keys, values, position, lengths[0], kv_local, group_heads)
    for section in range(sharing.bit_length() - 1):
        partner = partner_2((state[0], state[1], state[2]), "tp", section)
        state = join_softmax(state, partner)
    top, total, weighted = state
    steps = query.shape[0]
    heads = (weighted / total[..., None]).reshape(steps, kv_local * group_heads, HD)
    chosen = lax.dynamic_slice_in_dim(heads, segment * own_heads, own_heads, 1)
    attended = chosen.reshape(1, steps, own_heads * HD).astype(bf16)
    raw = jnp.concatenate([attended[0], history[0]], axis=0)
    rows_each = raw.shape[0]
    wide = raw.astype(f32)
    squares = lax.psum(jnp.sum(wide * wide, axis=-1), "tp")
    row_scale = lax.rsqrt(squares / D + 1e-05)
    scaled_rows = wide * row_scale[:, None] * norm_gain
    gathered = lax.all_gather(scaled_rows, "rep", axis=0, tiled=True)
    partial_value = jnp.dot(
        gathered, draft_weight, precision=lax.Precision.HIGHEST, preferred_element_type=f32
    )
    logits = lax.psum(partial_value, "tp")
    columns = draft_weight.shape[1]
    column_start = lax.axis_index("rep") * columns
    local_top = jnp.max(logits, axis=-1)
    local_total = jnp.sum(jnp.exp(logits - local_top[:, None]), axis=-1)
    top_all, total_all = merged((local_top, local_total), "rep", join_stats)
    probs = jnp.exp(logits - top_all[:, None]) / total_all[:, None]
    labels = column_start + jnp.arange(columns, dtype=jnp.int32)
    onehot = (targets.reshape(-1)[:, None] == labels[None, :]).astype(f32)
    keep = (
        (jnp.arange(rows_each, dtype=jnp.int32)[None, :] < accepted[:, None])
        .reshape(-1)
        .astype(f32)
    )
    delta = (probs - onehot) * keep[:, None]
    grad = jnp.dot(gathered.T, delta, precision=lax.Precision.HIGHEST, preferred_element_type=f32)
    return (attended, draft_weight - learn_rate * grad)


def exchange(value, axis, mask):
    pairs = [(source, source ^ mask) for source in range(lax.axis_size(axis))]
    return lax.ppermute(value, axis, pairs)


def whole(space=pltpu.VMEM):
    return pl.BlockSpec(memory_space=space)


def in_hbm(value):
    return pltpu.with_memory_space_constraint(value, pltpu.HBM)


def attention_kernel(
    kv_local,
    table_ref,
    length_ref,
    queries_ref,
    keys_ref,
    values_ref,
    history_ref,
    weight_ref,
    raw_ref,
    attended_ref,
    held_ref,
    query_buf,
    key_buf,
    value_buf,
    history_buf,
    query_sem,
    key_sem,
    value_sem,
    history_sem,
    weight_sem,
):
    pages, slots = keys_ref.shape[0], keys_ref.shape[1]
    steps = query_buf.shape[0]
    group = HQ // KVH
    span = query_buf.shape[1]
    start = pl.multiple_of(lax.axis_index("tp") * span, span)
    query_copy = pltpu.make_async_copy(queries_ref.at[:, pl.ds(start, span)], query_buf, query_sem)
    query_copy.start()
    key_copies, value_copies = [], []
    for source, target, sems, copies in (
        (keys_ref, key_buf, key_sem, key_copies),
        (values_ref, value_buf, value_sem, value_copies),
    ):
        for page in range(pages):
            copy = pltpu.make_async_copy(
                source.at[table_ref[page]], target.at[pl.ds(page * slots, slots)], sems.at[page]
            )
            copy.start()
            copies.append(copy)
    history_copy = pltpu.make_async_copy(history_ref, history_buf, history_sem)
    history_copy.start()
    query_copy.wait()
    queries = query_buf[...].astype(f32)
    stacked = []
    for head in range(kv_local):
        parts = [
            queries[:, (head * group + g) * HD : (head * group + g + 1) * HD] for g in range(group)
        ]
        stacked.append(jnp.concatenate(parts, axis=0).astype(bf16))
    for copy in key_copies + value_copies:
        copy.wait()
    weight_copies = column_copies(weight_ref, held_ref, weight_sem, 0)
    for copy in weight_copies:
        copy.start()
    shape = (group * steps, pages * slots)
    step = lax.broadcasted_iota(jnp.int32, shape, 0) % steps
    position = lax.broadcasted_iota(jnp.int32, shape, 1)
    valid = position <= length_ref[0] - steps + step
    expos, totals = [], []
    for head in range(kv_local):
        scores = lax.dot_general(
            stacked[head],
            key_buf[:, head * HD : (head + 1) * HD],
            (((1,), (1,)), ((), ())),
            preferred_element_type=f32,
        ) * (HD ** (-0.5))
        top = jnp.max(jnp.where(valid, scores, -1e30), axis=-1, keepdims=True)
        expo = jnp.where(valid, jnp.exp(scores - top), 0.0)
        totals.append(jnp.sum(expo, axis=-1, keepdims=True))
        expos.append(jnp.concatenate(split2(expo), axis=0))
    history_copy.wait()
    for head in range(kv_local):
        both = jnp.dot(
            expos[head],
            value_buf[:, head * HD : (head + 1) * HD],
            preferred_element_type=f32,
        )
        half = group * steps
        out = (both[:half] + both[half:]) / totals[head]
        for g in range(group):
            columns = slice((head * group + g) * HD, (head * group + g + 1) * HD)
            piece = out[g * steps : (g + 1) * steps]
            earlier = history_buf[:, columns].astype(f32)
            raw_ref[:, columns] = jnp.concatenate([piece, earlier], axis=0).astype(bf16)
            attended_ref[:, columns] = piece.astype(bf16)
    for copy in weight_copies:
        copy.wait()


def run_attention(queries, keys, values, table, length, history, weight, held):
    pages, slots, width = keys.shape
    kv_local = width // HD
    steps = queries.shape[0]
    span = kv_local * (HQ // KVH) * HD
    rows = steps + history.shape[0]
    return pl.pallas_call(
        functools.partial(attention_kernel, kv_local),
        out_shape=(
            jax.ShapeDtypeStruct((rows, span), bf16),
            jax.ShapeDtypeStruct((steps, span), bf16),
            pltpu.VMEM((weight.shape[0], held), f32),
        ),
        in_specs=[
            whole(pltpu.SMEM),
            whole(pltpu.SMEM),
            whole(pltpu.HBM),
            whole(pltpu.HBM),
            whole(pltpu.HBM),
            whole(pltpu.HBM),
            whole(pltpu.HBM),
        ],
        out_specs=(whole(), whole(), whole()),
        scratch_shapes=[
            pltpu.VMEM((steps, span), bf16),
            pltpu.VMEM((pages * slots, width), bf16),
            pltpu.VMEM((pages * slots, width), bf16),
            pltpu.VMEM(history.shape, bf16),
            pltpu.SemaphoreType.DMA,
            pltpu.SemaphoreType.DMA((pages,)),
            pltpu.SemaphoreType.DMA((pages,)),
            pltpu.SemaphoreType.DMA,
            pltpu.SemaphoreType.DMA((held // 256,)),
        ],
        compiler_params=pltpu.CompilerParams(vmem_limit_bytes=12 * MIB),
        cost_estimate=pl.CostEstimate(
            flops=4 * 64 * 1024 * 256, bytes_accessed=12 * MIB, transcendentals=131072
        ),
        name="attention",
    )(table, length, *(in_hbm(part) for part in (queries, keys, values, history, weight)))


def column_copies(source, target, sems, first, width=256):
    return [
        pltpu.make_async_copy(
            source.at[:, pl.ds(first + place, width)],
            target.at[:, pl.ds(place, width)],
            sems.at[index],
        )
        for index, place in enumerate(range(0, target.shape[1], width))
    ]


def load_kernel(first, count, weight_ref, token_ref, *refs):
    held_refs, done_ref, sems = refs[:count], refs[count], refs[count + 1]
    done_ref[...] = jnp.zeros(done_ref.shape, f32)
    copies = []
    for ref in held_refs:
        tiles = len(copies)
        copies += column_copies(weight_ref, ref, sems.at[pl.ds(tiles, ref.shape[1] // 256)], first)
        first += ref.shape[1]
    for copy in copies:
        copy.start()
    for copy in copies:
        copy.wait()


def run_load(weight, token, first, widths):
    rows = weight.shape[0]
    columns = sum(widths)
    *helds, done = pl.pallas_call(
        functools.partial(load_kernel, first, len(widths)),
        out_shape=tuple(pltpu.VMEM((rows, width), f32) for width in widths)
        + (jax.ShapeDtypeStruct((8, LANES), f32),),
        in_specs=[whole(pltpu.HBM), whole(pl.ANY)],
        out_specs=tuple(whole() for _ in range(len(widths) + 1)),
        scratch_shapes=[pltpu.SemaphoreType.DMA((columns // 256,))],
        compiler_params=pltpu.CompilerParams(vmem_limit_bytes=8 * MIB),
        cost_estimate=pl.CostEstimate(
            flops=0, bytes_accessed=4 * rows * columns, transcendentals=0
        ),
        name="load_weight",
    )(in_hbm(weight), token)
    return [pltpu.with_memory_space_constraint(held, pltpu.VMEM) for held in helds], done


def split2(value):
    high = value.astype(bf16)
    return high, (value - high.astype(f32)).astype(bf16)


def stack_kernel(*refs):
    each = refs[0].shape[0]
    for k, ref in enumerate(refs[:-2]):
        refs[-1][k * each : (k + 1) * each, :] = ref[...]


def run_stack(parts, after):
    each, features = parts[0].shape
    return pl.pallas_call(
        stack_kernel,
        out_shape=jax.ShapeDtypeStruct((len(parts) * each, features), bf16),
        in_specs=[whole() for _ in parts] + [whole(pl.ANY)],
        out_specs=whole(),
        compiler_params=pltpu.CompilerParams(vmem_limit_bytes=4 * MIB),
        cost_estimate=pl.CostEstimate(flops=4096, bytes_accessed=4096, transcendentals=0),
        name="stacked_rows",
    )(*parts, after)


def power_above(value):
    exponent = jnp.full(value.shape, -96.0, f32)
    for step in (128.0, 64.0, 32.0, 16.0, 8.0, 4.0, 2.0, 1.0):
        exponent = jnp.where(value > jnp.exp2(exponent + (step - 1.0)), exponent + step, exponent)
    return exponent


def logits_kernel(n_rep, n_tp, *refs):
    block_refs = refs[:2]
    gain_ref, *held_refs, weight_ref = refs[2:6]
    x_ref, own_ref, square_ref = refs[6:9]
    send_refs = refs[9 : 8 + n_tp]
    scaled_buf, partial_buf, rest_buf, rest_sem = refs[8 + n_tp :]
    tile = pl.program_id(0)
    rep, tp = lax.axis_index("rep"), lax.axis_index("tp")
    rows = x_ref.shape[0]
    each = rows // n_rep
    share = rows // n_tp
    width = partial_buf.shape[1] // pl.num_programs(0)
    held_columns = sum(ref.shape[1] for ref in held_refs)
    copies = column_copies(weight_ref, rest_buf, rest_sem, held_columns, width)

    @pl.when(tile == 0)
    def _():
        for copy in copies:
            copy.start()
        for k in range(n_rep):
            block = block_refs[k % 2][k // 2 * each : (k // 2 + 1) * each, :]
            place = pl.multiple_of(lax.bitwise_xor(rep, k) * each, each)
            x_ref[pl.ds(place, each), :] = block
            value = block.astype(f32)
            squares = jnp.sum(value * value, axis=-1, keepdims=True)
            square_ref[pl.ds(place, each), :] = jnp.broadcast_to(squares, (each, LANES))
            scaled_buf[pl.ds(place, each), :] = (value * gain_ref[...]).astype(bf16)

    columns = pl.ds(pl.multiple_of(tile * width, width), width)

    def multiply(weight):
        partial_buf[:, columns] = jnp.dot(
            scaled_buf[...], weight.astype(bf16), preferred_element_type=f32
        )

    first = 0
    for ref in held_refs:
        for index in range(ref.shape[1] // width):

            @pl.when(tile == first + index)
            def _():
                multiply(ref[:, index * width : (index + 1) * width])

        first += ref.shape[1] // width
    for index, copy in enumerate(copies):

        @pl.when(tile == first + index)
        def _():
            copy.wait()
            multiply(rest_buf[:, index * width : (index + 1) * width])

    @pl.when(tile == pl.num_programs(0) - 1)
    def _():
        own_ref[...] = partial_buf[pl.ds(pl.multiple_of(tp * share, share), share), :]
        full = partial_buf.shape[1]
        lane = lax.broadcasted_iota(jnp.int32, (share, LANES), 1)
        squares = jnp.zeros((share, LANES), f32)
        group = LANES // n_tp
        for j in range(n_tp):
            mine = (lane >= j * group) & (lane < (j + 1) * group)
            squares = jnp.where(mine, square_ref[j * share : (j + 1) * share, :], squares)
        first = jnp.floor(squares / 16.0)
        second = jnp.floor((squares - first * 16.0) * 2048.0)
        third = jnp.floor((squares - first * 16.0 - second / 2048.0) * 2.0**26)
        part = lane % group
        extra = jnp.where(part == 0, first, jnp.where(part == 1, second, third))
        for k in range(1, n_tp):
            place = pl.multiple_of(lax.bitwise_xor(tp, k) * share, share)
            value = partial_buf[pl.ds(place, share), :]
            exponent = power_above(jnp.max(jnp.abs(value), axis=-1, keepdims=True))
            coded = jnp.floor(value * jnp.exp2(15.0 - exponent) + 0.5)
            coded = jnp.clip(coded, -32768.0, 32767.0)
            send_refs[k - 1][:, :full] = coded.astype(jnp.int32).astype(jnp.int16)
            tail = jnp.where(part == 3, exponent, extra)
            send_refs[k - 1][:, full:] = tail.astype(jnp.int32).astype(jnp.int16)


def run_logits(blocks, gain, helds, weight, n_rep, n_tp):
    rows, features = 2 * blocks[0].shape[0], blocks[0].shape[1]
    columns = weight.shape[1]
    share = rows // n_tp
    tiles = columns // TILE
    rest = columns - sum(held.shape[1] for held in helds)
    return pl.pallas_call(
        functools.partial(logits_kernel, n_rep, n_tp),
        grid=(tiles,),
        out_shape=(
            jax.ShapeDtypeStruct((rows, features), bf16),
            jax.ShapeDtypeStruct((share, columns), f32),
            jax.ShapeDtypeStruct((rows, LANES), f32),
        )
        + tuple(
            jax.ShapeDtypeStruct((share, columns + LANES), jnp.int16) for _ in range(n_tp - 1)
        ),
        in_specs=[whole() for _ in range(3 + len(helds))] + [whole(pltpu.HBM)],
        out_specs=tuple(whole() for _ in range(n_tp + 2)),
        scratch_shapes=[
            pltpu.VMEM((rows, features), bf16),
            pltpu.VMEM((rows, columns), f32),
            pltpu.VMEM((features, rest), f32),
            pltpu.SemaphoreType.DMA((rest // TILE,)),
        ],
        compiler_params=pltpu.CompilerParams(vmem_limit_bytes=14 * MIB),
        cost_estimate=pl.CostEstimate(
            flops=6 * rows * features * columns,
            bytes_accessed=4 * features * columns,
            transcendentals=0,
        ),
        name="partial_logits",
    )(*blocks, gain, *helds, in_hbm(weight))


def decoded(ref, columns):
    share = ref.shape[0]
    tail = ref[:, columns:].astype(jnp.int32).astype(f32)
    part = lax.broadcasted_iota(jnp.int32, (share, LANES), 1) % (LANES // lax.axis_size("tp"))
    unit = jnp.where(part == 0, 16.0, jnp.where(part == 1, 1.0 / 2048.0, 2.0**-26))
    unit = jnp.where(part < 3, unit, 0.0)
    value = ref[:, :columns].astype(jnp.int32).astype(f32)
    return value * jnp.exp2(tail[:, 3:4] - 15.0), tail * unit


def softmax_kernel(n_tp, n_more, own_ref, square_ref, *refs):
    received = refs[: n_tp - 1]
    left_ref, right_ref, scale_ref = refs[n_tp - 1 + n_more : n_tp + 2 + n_more]
    share, columns = own_ref.shape
    group = LANES // n_tp
    lane = lax.broadcasted_iota(jnp.int32, (share, LANES), 1)
    logits, squares = own_ref[...], jnp.zeros((share, LANES), f32)
    for ref in received:
        value, more = decoded(ref, columns)
        logits, squares = logits + value, squares + more
    for j in range(n_tp):
        rows = slice(j * share, (j + 1) * share)
        mine = jnp.where((lane >= j * group) & (lane < (j + 1) * group), squares, 0.0)
        total = square_ref[rows, :] + jnp.sum(mine, axis=-1, keepdims=True)
        scale_ref[rows, :] = lax.rsqrt(total / D + 1e-05)
    tp = lax.axis_index("tp")
    scale = scale_ref[pl.ds(pl.multiple_of(tp * share, share), share), :]
    logits = logits * scale[:, :1]
    top = jnp.max(logits, axis=-1, keepdims=True)
    expo = jnp.exp(logits - top)
    total = jnp.sum(expo, axis=-1, keepdims=True)
    width = right_ref.shape[1]
    place = columns - width
    left_ref[:, :place] = expo[:, :place].astype(bf16)
    right_ref[...] = expo[:, place:].astype(bf16)
    for value in (top, total):
        for _ in range(3):
            high = value.astype(bf16)
            left_ref[:, place : place + 1] = high
            value = value - high.astype(f32)
            place += 1


def held_shapes(helds):
    return tuple(pltpu.VMEM(held.shape, f32) for held in helds)


def run_softmax(own, squares, received, after, helds):
    share, columns = own.shape
    rows = squares.shape[0]
    return pl.pallas_call(
        functools.partial(softmax_kernel, len(received) + 1, len(after) + len(helds)),
        out_shape=(
            jax.ShapeDtypeStruct((share, AGAIN[0] + LANES), bf16),
            jax.ShapeDtypeStruct((share, columns - AGAIN[0]), bf16),
            jax.ShapeDtypeStruct((rows, LANES), f32),
        )
        + held_shapes(helds),
        in_specs=[whole() for _ in range(len(received) + 2)] + [whole(pl.ANY) for _ in after]
        + [whole() for _ in helds],
        out_specs=tuple(whole() for _ in range(3 + len(helds))),
        input_output_aliases={len(received) + len(after) + 2 + i: 3 + i for i in range(len(helds))},
        compiler_params=pltpu.CompilerParams(vmem_limit_bytes=8 * MIB),
        cost_estimate=pl.CostEstimate(flops=65536, bytes_accessed=65536, transcendentals=0),
        name="local_softmax",
    )(own, squares, *received, *after, *helds)


def stats_kernel(n_tp, n_held, *refs):
    stats, out_ref, column_buf = refs[:n_tp], refs[n_tp + n_held], refs[-1]
    share = stats[0].shape[0]
    tp = lax.axis_index("tp")
    lane = lax.broadcasted_iota(jnp.int32, (share, LANES), 1)
    for k, ref in zip((0, *BACK_ORDER), stats):
        parts = ref[:, ref.shape[1] - LANES :].astype(f32)
        top = parts[:, 0:1] + parts[:, 1:2] + parts[:, 2:3]
        total = parts[:, 3:4] + parts[:, 4:5] + parts[:, 5:6]
        place = pl.multiple_of(lax.bitwise_xor(tp, k) * share, share)
        column_buf[pl.ds(place, share), :] = jnp.where(lane == 0, top, total)
    out_ref[...] = column_buf[...].T[:8, :]


def run_stats(lefts, helds):
    rows = len(lefts) * lefts[0].shape[0]
    return pl.pallas_call(
        functools.partial(stats_kernel, len(lefts), len(helds)),
        out_shape=(jax.ShapeDtypeStruct((8, rows), f32),) + held_shapes(helds),
        in_specs=[whole() for _ in range(len(lefts) + len(helds))],
        out_specs=tuple(whole() for _ in range(1 + len(helds))),
        input_output_aliases={len(lefts) + i: 1 + i for i in range(len(helds))},
        scratch_shapes=[pltpu.VMEM((rows, LANES), f32)],
        compiler_params=pltpu.CompilerParams(vmem_limit_bytes=8 * MIB),
        cost_estimate=pl.CostEstimate(flops=65536, bytes_accessed=65536, transcendentals=0),
        name="row_stats",
    )(*lefts, *helds)


def joined(stats):
    top = stats[0][0:1, :]
    for ref in stats[1:]:
        top = jnp.maximum(top, ref[0:1, :])
    total = jnp.zeros_like(top)
    for ref in stats:
        total = total + ref[1:2, :] * jnp.exp(ref[0:1, :] - top)
    return top, total


def join_kernel(first_ref, second_ref, out_ref):
    top, total = joined((first_ref, second_ref))
    row = lax.broadcasted_iota(jnp.int32, out_ref.shape, 0)
    out_ref[...] = jnp.where(row == 0, top, total)


def run_join(first, second):
    return pl.pallas_call(
        join_kernel,
        out_shape=jax.ShapeDtypeStruct(first.shape, f32),
        in_specs=[whole(), whole()],
        out_specs=whole(),
        compiler_params=pltpu.CompilerParams(vmem_limit_bytes=4 * MIB),
        cost_estimate=pl.CostEstimate(flops=4096, bytes_accessed=4096, transcendentals=0),
        name="pair_stats",
    )(first, second)


def turn_kernel(x_ref, gain_ref, out_ref):
    out_ref[...] = (x_ref[...].astype(f32) * gain_ref[...]).T


def run_turn(x, gain):
    rows, features = x.shape
    tile = 1024
    return pl.pallas_call(
        turn_kernel,
        grid=(features // tile,),
        out_shape=jax.ShapeDtypeStruct((features, rows), f32),
        in_specs=[
            pl.BlockSpec((rows, tile), lambda i: (0, i)),
            pl.BlockSpec((1, tile), lambda i: (0, i)),
        ],
        out_specs=pl.BlockSpec((tile, rows), lambda i: (i, 0)),
        compiler_params=pltpu.CompilerParams(vmem_limit_bytes=8 * MIB),
        cost_estimate=pl.CostEstimate(flops=4096, bytes_accessed=4096, transcendentals=0),
        name="turned_rows",
    )(x, gain)


def scale_kernel(
    n_held, first, turned_ref, scale_ref, targets_ref, accepted_ref, weight_ref, *refs
):
    out_ref, target_ref = refs[n_held : n_held + 2]
    rest_ref, sems = refs[-2:]
    copies = column_copies(weight_ref, rest_ref, sems, first)
    for copy in copies:
        copy.start()
    rows = turned_ref.shape[1]
    scale = scale_ref[...].T[:1, :] * learn_rate
    high, low = split2(turned_ref[...] * scale)
    out_ref[:, :rows] = high
    out_ref[:, rows:] = low
    each = targets_ref.shape[1]
    row = lax.broadcasted_iota(jnp.int32, (each, LANES), 0)
    for block in range(rows // each):
        target = jnp.zeros((each, LANES), jnp.int32)
        for i in range(each):
            target = jnp.where(row == i, targets_ref[block, i], target)
        target = jnp.where(row < accepted_ref[block], target, -1)
        target_ref[block * each : (block + 1) * each, :] = target
    for copy in copies:
        copy.wait()


def run_scale(turned, scale, targets, accepted, weight, helds):
    features, rows = turned.shape
    first = sum(held.shape[1] for held in helds)
    rest = weight.shape[1] - first
    return pl.pallas_call(
        functools.partial(scale_kernel, len(helds), first),
        out_shape=(
            jax.ShapeDtypeStruct((features, 2 * rows), bf16),
            jax.ShapeDtypeStruct((rows, LANES), jnp.int32),
        )
        + held_shapes(helds)
        + (pltpu.VMEM((features, rest), f32),),
        in_specs=[
            whole(),
            whole(),
            whole(pltpu.SMEM),
            whole(pltpu.SMEM),
            whole(pltpu.HBM),
        ]
        + [whole() for _ in helds],
        out_specs=tuple(whole() for _ in range(3 + len(helds))),
        input_output_aliases={5 + i: 2 + i for i in range(len(helds))},
        scratch_shapes=[pltpu.SemaphoreType.DMA((rest // 256,))],
        compiler_params=pltpu.CompilerParams(vmem_limit_bytes=8 * MIB),
        cost_estimate=pl.CostEstimate(flops=65536, bytes_accessed=65536, transcendentals=0),
        name="scaled_rows",
    )(turned, scale, targets, accepted, in_hbm(weight), *helds)


def update_kernel(n_tp, n_held, n_kept, first, total_columns, *refs):
    turned_ref, target_ref = refs[:2]
    expo_refs = refs[2 : 2 + n_tp]
    own_stat_ref, *stat_refs = refs[2 + n_tp : 3 + 2 * n_tp]
    out_ref, *held_refs = refs[-4 - n_held - n_kept : -3 - n_kept]
    delta_buf, factor_buf, sems = refs[-3:]
    rep, tp = lax.axis_index("rep"), lax.axis_index("tp")
    share = expo_refs[0].shape[0]
    rows, columns = n_tp * share, delta_buf.shape[1]
    top, total = joined(stat_refs)
    factor = jnp.exp(own_stat_ref[0:1, :] - top) / total
    factor = jnp.broadcast_to(factor, (rows, rows)).T
    trained = jnp.where(target_ref[...] >= 0, 1.0, 0.0)
    factor_buf[...] = factor[:, :LANES] * trained
    label = lax.broadcasted_iota(jnp.int32, (share, columns), 1) + (rep * total_columns + first)
    for k, ref in zip((0, *BACK_ORDER), expo_refs):
        place = pl.multiple_of(lax.bitwise_xor(tp, k) * share, share)
        mine = pl.ds(place, share)
        onehot = jnp.where(label == target_ref[mine, 0:1], 1.0, 0.0)
        delta = ref[:, :columns].astype(f32) * factor_buf[mine, 0:1] - onehot
        delta = delta.astype(bf16)
        delta_buf[mine, :] = delta
        delta_buf[pl.ds(pl.multiple_of(rows + place, share), share), :] = delta

    height = HEIGHT
    steps = turned_ref.shape[0] // height

    def copies_of(step):
        mine = pl.ds(pl.multiple_of(step * height, height), height)
        place, copies = first, []
        for index, ref in enumerate(held_refs):
            target = out_ref.at[mine, pl.ds(place, ref.shape[1])]
            copies.append(pltpu.make_async_copy(ref.at[mine], target, sems.at[index, step]))
            place += ref.shape[1]
        return copies

    def one_step(step, _):
        mine = pl.ds(pl.multiple_of(step * height, height), height)
        grad = jnp.dot(turned_ref[mine, :], delta_buf[...], preferred_element_type=f32)
        place = 0
        for ref in held_refs:
            ref[mine, :] = ref[mine, :] - grad[:, place : place + ref.shape[1]]
            place += ref.shape[1]
        for copy in copies_of(step):
            copy.start()
        return 0

    def one_wait(step, _):
        for copy in copies_of(step):
            copy.wait()
        return 0

    lax.fori_loop(0, steps, one_step, 0)
    lax.fori_loop(0, steps, one_wait, 0)


def run_update(turned, target, expos, stats, helds, kept, first, total_columns, out=None):
    features, pair = turned.shape
    columns = sum(held.shape[1] for held in helds)
    n_tp, n_held = len(expos), len(helds)
    earlier = () if out is None else (out,)
    pieces = (*helds, *kept)
    inputs = (turned, target, *expos, *stats)
    before = len(inputs) + len(earlier)
    aliases = {before + i: 1 + i for i in range(len(pieces))}
    if earlier:
        aliases[len(inputs)] = 0
    new_weight, *pieces = pl.pallas_call(
        functools.partial(update_kernel, n_tp, n_held, len(kept), first, total_columns),
        out_shape=(jax.ShapeDtypeStruct((features, total_columns), f32),) + held_shapes(pieces),
        in_specs=[whole() for _ in inputs]
        + [whole(pltpu.HBM) for _ in earlier]
        + [whole() for _ in pieces],
        out_specs=(whole(pltpu.HBM),) + tuple(whole() for _ in pieces),
        input_output_aliases=aliases,
        scratch_shapes=[
            pltpu.VMEM((pair, columns), bf16),
            pltpu.VMEM((pair // 2, LANES), f32),
            pltpu.SemaphoreType.DMA((n_held, features // HEIGHT)),
        ],
        compiler_params=pltpu.CompilerParams(vmem_limit_bytes=10 * MIB),
        cost_estimate=pl.CostEstimate(
            flops=2 * pair * features * columns,
            bytes_accessed=4 * features * columns,
            transcendentals=0,
        ),
        name="weight_update",
    )(*inputs, *earlier, *pieces)
    return new_weight, pieces[n_held:]


def direct_plan(
    queries,
    cache_keys,
    cache_values,
    page_table,
    lengths,
    history,
    norm_gain,
    draft_weight,
    targets,
    accepted,
):
    n_rep, n_tp = lax.axis_size("rep"), lax.axis_size("tp")
    gain = norm_gain.reshape(1, -1)
    raw, attended, first = run_attention(
        queries[0],
        cache_keys[0, 0],
        cache_values[0, 0],
        page_table[0, 0],
        lengths,
        history[0],
        draft_weight,
        HELD[0],
    )
    first = pltpu.with_memory_space_constraint(first, pltpu.VMEM)
    (second,), loaded = run_load(draft_weight, raw, HELD[0], HELD[1:])
    raws = [raw] + [exchange(raw, "rep", k) for k in range(2, n_rep, 2)]
    block = run_stack(raws, loaded)
    blocks = (block, exchange(block, "rep", 1))
    x, own, squares, *sends = run_logits(
        blocks, gain, (first, second), draft_weight, n_rep, n_tp
    )
    turned = run_turn(x, gain)
    received = [exchange(sends[k - 1], "tp", k) for k in SUM_ORDER]
    helds, loaded = run_load(draft_weight, own, 0, AGAIN)
    left, right, scale, *helds = run_softmax(own, squares, received, (loaded, turned), helds)
    lefts = [left] + [exchange(left, "tp", k) for k in BACK_ORDER]
    scaled, target, *helds = run_scale(turned, scale, targets, accepted, draft_weight, helds)
    stat, *helds = run_stats(lefts, helds)
    pair = run_join(stat, exchange(stat, "rep", 1))
    stats = [stat, pair] + [exchange(pair, "rep", k) for k in range(2, n_rep, 2)]
    helds = [pltpu.with_memory_space_constraint(held, pltpu.VMEM) for held in helds]
    columns = draft_weight.shape[1]
    new_weight, kept = run_update(
        scaled, target, lefts, stats, helds[:1], helds[1:], 0, columns
    )
    kept = [pltpu.with_memory_space_constraint(held, pltpu.VMEM) for held in kept]
    rights = [right] + [exchange(right, "tp", k) for k in BACK_ORDER]
    new_weight, _ = run_update(
        scaled, target, rights, stats, kept, (), AGAIN[0], columns, new_weight
    )
    return (attended[None], new_weight)


def solution(mesh):
    plan = direct_plan if (mesh.shape["rep"], mesh.shape["tp"]) == (8, 4) else general_plan
    return jax.shard_map(
        plan,
        mesh=mesh,
        in_specs=(
            P("rep", None, None),
            P("rep", "tp", None, None, None),
            P("rep", "tp", None, None, None),
            P("rep", "tp", None),
            P("rep"),
            P("rep", None, "tp"),
            P("tp"),
            P("tp", "rep"),
            P(),
            P(),
        ),
        out_specs=(P("rep", None, "tp"), P("tp", "rep")),
        check_vma=False,
    )
```

```python
import functools

import jax
import jax.numpy as jnp
from jax import lax
from jax.experimental import pallas as pl
from jax.experimental.pallas import tpu as pltpu
from jax.sharding import PartitionSpec as P

HQ = 128
KVH = 8
HD = 128
D = 16384

learn_rate = 0.5
LANES = 128
MIB = 1024 * 1024
TILE = 512
SUM_ORDER = (2, 1, 3)
BACK_ORDER = (1, 2, 3)
HEIGHT = 512
HELD = (512, 1024)
AGAIN = (768, 1024)
bf16 = jnp.bfloat16
f32 = jnp.float32


def partner_2(value, axis, distance):
    mask = 2**distance
    pairs = [(source, source ^ mask) for source in range(lax.axis_size(axis))]
    return lax.ppermute(value, axis, pairs)


def merged(value, axis, join):
    pieces = jax.tree.map(lambda part: lax.all_gather(part, axis), value)
    head = jax.tree.map(lambda part: part[0], pieces)
    tail = jax.tree.map(lambda part: part[1:], pieces)
    so_far, _ = lax.scan(lambda so_far, share: (join(so_far, share), None), head, tail)
    return so_far


def attend(query, keys, values, position, length, kv_local, group_heads):
    steps = query.shape[0]
    limit = length - steps + jnp.arange(steps, dtype=jnp.int32)
    valid = (position[None, :] <= limit[:, None])[:, None, None, :]
    grouped = query.astype(f32).reshape(steps, kv_local, group_heads, HD)
    scores = jnp.einsum("skgd,pkd->skgp", grouped, keys.astype(f32)) * HD ** (-0.5)
    top = jnp.max(jnp.where(valid, scores, -1e30), axis=-1)
    expo = jnp.where(valid, jnp.exp(scores - top[..., None]), 0.0)
    total = jnp.sum(expo, axis=-1)
    weighted = jnp.einsum("skgp,pkd->skgd", expo, values.astype(f32))
    return (top, total, weighted)


def join_softmax(first, second):
    top = jnp.maximum(first[0], second[0])
    left = jnp.exp(first[0] - top)
    right = jnp.exp(second[0] - top)
    return (
        top,
        first[1] * left + second[1] * right,
        first[2] * left[..., None] + second[2] * right[..., None],
    )


def join_stats(first, second):
    top = jnp.maximum(first[0], second[0])
    return (top, first[1] * jnp.exp(first[0] - top) + second[1] * jnp.exp(second[0] - top))


def general_plan(
    queries,
    cache_keys,
    cache_values,
    page_table,
    lengths,
    history,
    norm_gain,
    draft_weight,
    targets,
    accepted,
):
    owner = lax.axis_index("tp")
    owners = lax.axis_size("tp")
    kv_local = cache_keys.shape[4] // HD
    sharing = max(1, owners // KVH)
    group_heads = HQ // KVH
    own_heads = HQ // owners
    segment = owner % sharing
    first_head = owner // sharing * kv_local
    table = page_table[0, 0]
    keys = cache_keys[0, 0][table].reshape(-1, kv_local, HD)
    values = cache_values[0, 0][table].reshape(-1, kv_local, HD)
    pages = table.shape[0]
    slots = cache_keys.shape[3]
    position = (
        (jnp.arange(pages, dtype=jnp.int32)[:, None] * sharing + segment) * slots
        + jnp.arange(slots, dtype=jnp.int32)[None, :]
    ).reshape(-1)
    span = kv_local * group_heads * HD
    query = lax.dynamic_slice_in_dim(queries[0], first_head * group_heads * HD, span, 1)
    state = attend(query, keys, values, position, lengths[0], kv_local, group_heads)
    for section in range(sharing.bit_length() - 1):
        partner = partner_2((state[0], state[1], state[2]), "tp", section)
        state = join_softmax(state, partner)
    top, total, weighted = state
    steps = query.shape[0]
    heads = (weighted / total[..., None]).reshape(steps, kv_local * group_heads, HD)
    chosen = lax.dynamic_slice_in_dim(heads, segment * own_heads, own_heads, 1)
    attended = chosen.reshape(1, steps, own_heads * HD).astype(bf16)
    raw = jnp.concatenate([attended[0], history[0]], axis=0)
    rows_each = raw.shape[0]
    wide = raw.astype(f32)
    squares = lax.psum(jnp.sum(wide * wide, axis=-1), "tp")
    row_scale = lax.rsqrt(squares / D + 1e-05)
    scaled_rows = wide * row_scale[:, None] * norm_gain
    gathered = lax.all_gather(scaled_rows, "rep", axis=0, tiled=True)
    partial_value = jnp.dot(
        gathered, draft_weight, precision=lax.Precision.HIGHEST, preferred_element_type=f32
    )
    logits = lax.psum(partial_value, "tp")
    columns = draft_weight.shape[1]
    column_start = lax.axis_index("rep") * columns
    local_top = jnp.max(logits, axis=-1)
    local_total = jnp.sum(jnp.exp(logits - local_top[:, None]), axis=-1)
    top_all, total_all = merged((local_top, local_total), "rep", join_stats)
    probs = jnp.exp(logits - top_all[:, None]) / total_all[:, None]
    labels = column_start + jnp.arange(columns, dtype=jnp.int32)
    onehot = (targets.reshape(-1)[:, None] == labels[None, :]).astype(f32)
    keep = (
        (jnp.arange(rows_each, dtype=jnp.int32)[None, :] < accepted[:, None])
        .reshape(-1)
        .astype(f32)
    )
    delta = (probs - onehot) * keep[:, None]
    grad = jnp.dot(gathered.T, delta, precision=lax.Precision.HIGHEST, preferred_element_type=f32)
    return (attended, draft_weight - learn_rate * grad)


def exchange(value, axis, mask):
    pairs = [(source, source ^ mask) for source in range(lax.axis_size(axis))]
    return lax.ppermute(value, axis, pairs)


def whole(space=pltpu.VMEM):
    return pl.BlockSpec(memory_space=space)


def in_hbm(value):
    return pltpu.with_memory_space_constraint(value, pltpu.HBM)


def attention_kernel(
    kv_local,
    table_ref,
    length_ref,
    queries_ref,
    keys_ref,
    values_ref,
    history_ref,
    weight_ref,
    raw_ref,
    attended_ref,
    held_ref,
    query_buf,
    key_buf,
    value_buf,
    history_buf,
    query_sem,
    key_sem,
    value_sem,
    history_sem,
    weight_sem,
):
    pages, slots = keys_ref.shape[0], keys_ref.shape[1]
    steps = query_buf.shape[0]
    group = HQ // KVH
    span = query_buf.shape[1]
    start = pl.multiple_of(lax.axis_index("tp") * span, span)
    weight_copies = column_copies(weight_ref, held_ref, weight_sem, 0)
    for copy in weight_copies:
        copy.start()
    query_copy = pltpu.make_async_copy(queries_ref.at[:, pl.ds(start, span)], query_buf, query_sem)
    query_copy.start()
    key_copies, value_copies = [], []
    for source, target, sems, copies in (
        (keys_ref, key_buf, key_sem, key_copies),
        (values_ref, value_buf, value_sem, value_copies),
    ):
        for page in range(pages):
            copy = pltpu.make_async_copy(
                source.at[table_ref[page]], target.at[pl.ds(page * slots, slots)], sems.at[page]
            )
            copy.start()
            copies.append(copy)
    history_copy = pltpu.make_async_copy(history_ref, history_buf, history_sem)
    history_copy.start()
    query_copy.wait()
    queries = query_buf[...].astype(f32)
    stacked = []
    for head in range(kv_local):
        parts = [
            queries[:, (head * group + g) * HD : (head * group + g + 1) * HD] for g in range(group)
        ]
        stacked.append(jnp.concatenate(parts, axis=0).astype(bf16))
    for copy in key_copies:
        copy.wait()
    shape = (group * steps, pages * slots)
    step = lax.broadcasted_iota(jnp.int32, shape, 0) % steps
    position = lax.broadcasted_iota(jnp.int32, shape, 1)
    valid = position <= length_ref[0] - steps + step
    expos, totals = [], []
    for head in range(kv_local):
        scores = lax.dot_general(
            stacked[head],
            key_buf[:, head * HD : (head + 1) * HD],
            (((1,), (1,)), ((), ())),
            preferred_element_type=f32,
        ) * (HD ** (-0.5))
        top = jnp.max(jnp.where(valid, scores, -1e30), axis=-1, keepdims=True)
        expo = jnp.where(valid, jnp.exp(scores - top), 0.0)
        totals.append(jnp.sum(expo, axis=-1, keepdims=True))
        expos.append(jnp.concatenate(split2(expo), axis=0))
    for copy in value_copies:
        copy.wait()
    history_copy.wait()
    for head in range(kv_local):
        both = jnp.dot(
            expos[head],
            value_buf[:, head * HD : (head + 1) * HD],
            preferred_element_type=f32,
        )
        half = group * steps
        out = (both[:half] + both[half:]) / totals[head]
        for g in range(group):
            columns = slice((head * group + g) * HD, (head * group + g + 1) * HD)
            piece = out[g * steps : (g + 1) * steps]
            earlier = history_buf[:, columns].astype(f32)
            raw_ref[:, columns] = jnp.concatenate([piece, earlier], axis=0).astype(bf16)
            attended_ref[:, columns] = piece.astype(bf16)
    for copy in weight_copies:
        copy.wait()


def run_attention(queries, keys, values, table, length, history, weight, held):
    pages, slots, width = keys.shape
    kv_local = width // HD
    steps = queries.shape[0]
    span = kv_local * (HQ // KVH) * HD
    rows = steps + history.shape[0]
    return pl.pallas_call(
        functools.partial(attention_kernel, kv_local),
        out_shape=(
            jax.ShapeDtypeStruct((rows, span), bf16),
            jax.ShapeDtypeStruct((steps, span), bf16),
            pltpu.VMEM((weight.shape[0], held), f32),
        ),
        in_specs=[
            whole(pltpu.SMEM),
            whole(pltpu.SMEM),
            whole(pltpu.HBM),
            whole(pltpu.HBM),
            whole(pltpu.HBM),
            whole(pltpu.HBM),
            whole(pltpu.HBM),
        ],
        out_specs=(whole(), whole(), whole()),
        scratch_shapes=[
            pltpu.VMEM((steps, span), bf16),
            pltpu.VMEM((pages * slots, width), bf16),
            pltpu.VMEM((pages * slots, width), bf16),
            pltpu.VMEM(history.shape, bf16),
            pltpu.SemaphoreType.DMA,
            pltpu.SemaphoreType.DMA((pages,)),
            pltpu.SemaphoreType.DMA((pages,)),
            pltpu.SemaphoreType.DMA,
            pltpu.SemaphoreType.DMA((held // 256,)),
        ],
        compiler_params=pltpu.CompilerParams(vmem_limit_bytes=12 * MIB),
        cost_estimate=pl.CostEstimate(
            flops=4 * 64 * 1024 * 256, bytes_accessed=12 * MIB, transcendentals=131072
        ),
        name="attention",
    )(in_hbm(table), length, *(in_hbm(part) for part in (queries, keys, values, history, weight)))


def column_copies(source, target, sems, first, width=256):
    return [
        pltpu.make_async_copy(
            source.at[:, pl.ds(first + place, width)],
            target.at[:, pl.ds(place, width)],
            sems.at[index],
        )
        for index, place in enumerate(range(0, target.shape[1], width))
    ]


def load_kernel(first, count, weight_ref, token_ref, *refs):
    held_refs, done_ref, sems = refs[:count], refs[count], refs[count + 1]
    done_ref[...] = jnp.zeros(done_ref.shape, f32)
    copies = []
    for ref in held_refs:
        tiles = len(copies)
        copies += column_copies(weight_ref, ref, sems.at[pl.ds(tiles, ref.shape[1] // 256)], first)
        first += ref.shape[1]
    for copy in copies:
        copy.start()
    for copy in copies:
        copy.wait()


def run_load(weight, token, first, widths):
    rows = weight.shape[0]
    columns = sum(widths)
    *helds, done = pl.pallas_call(
        functools.partial(load_kernel, first, len(widths)),
        out_shape=tuple(pltpu.VMEM((rows, width), f32) for width in widths)
        + (jax.ShapeDtypeStruct((8, LANES), f32),),
        in_specs=[whole(pltpu.HBM), whole(pl.ANY)],
        out_specs=tuple(whole() for _ in range(len(widths) + 1)),
        scratch_shapes=[pltpu.SemaphoreType.DMA((columns // 256,))],
        compiler_params=pltpu.CompilerParams(vmem_limit_bytes=8 * MIB),
        cost_estimate=pl.CostEstimate(
            flops=0, bytes_accessed=4 * rows * columns, transcendentals=0
        ),
        name="load_weight",
    )(in_hbm(weight), token)
    return [pltpu.with_memory_space_constraint(held, pltpu.VMEM) for held in helds], done


def split2(value):
    high = value.astype(bf16)
    return high, (value - high.astype(f32)).astype(bf16)


def stack_kernel(*refs):
    each = refs[0].shape[0]
    for k, ref in enumerate(refs[:-2]):
        refs[-1][k * each : (k + 1) * each, :] = ref[...]


def run_stack(parts, after):
    each, features = parts[0].shape
    return pl.pallas_call(
        stack_kernel,
        out_shape=jax.ShapeDtypeStruct((len(parts) * each, features), bf16),
        in_specs=[whole() for _ in parts] + [whole(pl.ANY)],
        out_specs=whole(),
        compiler_params=pltpu.CompilerParams(vmem_limit_bytes=4 * MIB),
        cost_estimate=pl.CostEstimate(flops=4096, bytes_accessed=4096, transcendentals=0),
        name="stacked_rows",
    )(*parts, after)


def power_above(value):
    exponent = jnp.full(value.shape, -96.0, f32)
    for step in (128.0, 64.0, 32.0, 16.0, 8.0, 4.0, 2.0, 1.0):
        exponent = jnp.where(value > jnp.exp2(exponent + (step - 1.0)), exponent + step, exponent)
    return exponent


def logits_kernel(n_rep, n_tp, *refs):
    block_refs = refs[:2]
    gain_ref, *held_refs, weight_ref = refs[2:6]
    x_ref, own_ref, square_ref = refs[6:9]
    send_refs = refs[9 : 8 + n_tp]
    scaled_buf, partial_buf, rest_buf, rest_sem = refs[8 + n_tp :]
    tile = pl.program_id(0)
    rep, tp = lax.axis_index("rep"), lax.axis_index("tp")
    rows = x_ref.shape[0]
    each = rows // n_rep
    share = rows // n_tp
    width = partial_buf.shape[1] // pl.num_programs(0)
    held_columns = sum(ref.shape[1] for ref in held_refs)
    copies = column_copies(weight_ref, rest_buf, rest_sem, held_columns, width)

    @pl.when(tile == 0)
    def _():
        for copy in copies:
            copy.start()
        for k in range(n_rep):
            block = block_refs[k % 2][k // 2 * each : (k // 2 + 1) * each, :]
            place = pl.multiple_of(lax.bitwise_xor(rep, k) * each, each)
            x_ref[pl.ds(place, each), :] = block
            value = block.astype(f32)
            squares = jnp.sum(value * value, axis=-1, keepdims=True)
            square_ref[pl.ds(place, each), :] = jnp.broadcast_to(squares, (each, LANES))
            scaled_buf[pl.ds(place, each), :] = (value * gain_ref[...]).astype(bf16)

    columns = pl.ds(pl.multiple_of(tile * width, width), width)

    def multiply(weight):
        partial_buf[:, columns] = jnp.dot(
            scaled_buf[...], weight.astype(bf16), preferred_element_type=f32
        )

    first = 0
    for ref in held_refs:
        for index in range(ref.shape[1] // width):

            @pl.when(tile == first + index)
            def _():
                multiply(ref[:, index * width : (index + 1) * width])

        first += ref.shape[1] // width
    for index, copy in enumerate(copies):

        @pl.when(tile == first + index)
        def _():
            copy.wait()
            multiply(rest_buf[:, index * width : (index + 1) * width])

    @pl.when(tile == pl.num_programs(0) - 1)
    def _():
        own_ref[...] = partial_buf[pl.ds(pl.multiple_of(tp * share, share), share), :]
        full = partial_buf.shape[1]
        lane = lax.broadcasted_iota(jnp.int32, (share, LANES), 1)
        squares = jnp.zeros((share, LANES), f32)
        group = LANES // n_tp
        for j in range(n_tp):
            mine = (lane >= j * group) & (lane < (j + 1) * group)
            squares = jnp.where(mine, square_ref[j * share : (j + 1) * share, :], squares)
        first = jnp.floor(squares / 16.0)
        second = jnp.floor((squares - first * 16.0) * 2048.0)
        third = jnp.floor((squares - first * 16.0 - second / 2048.0) * 2.0**26)
        part = lane % group
        extra = jnp.where(part == 0, first, jnp.where(part == 1, second, third))
        for k in range(1, n_tp):
            place = pl.multiple_of(lax.bitwise_xor(tp, k) * share, share)
            value = partial_buf[pl.ds(place, share), :]
            exponent = power_above(jnp.max(jnp.abs(value), axis=-1, keepdims=True))
            coded = jnp.floor(value * jnp.exp2(15.0 - exponent) + 0.5)
            coded = jnp.clip(coded, -32768.0, 32767.0)
            send_refs[k - 1][:, :full] = coded.astype(jnp.int32).astype(jnp.int16)
            tail = jnp.where(part == 3, exponent, extra)
            send_refs[k - 1][:, full:] = tail.astype(jnp.int32).astype(jnp.int16)


def run_logits(blocks, gain, helds, weight, n_rep, n_tp):
    rows, features = 2 * blocks[0].shape[0], blocks[0].shape[1]
    columns = weight.shape[1]
    share = rows // n_tp
    tiles = columns // TILE
    rest = columns - sum(held.shape[1] for held in helds)
    return pl.pallas_call(
        functools.partial(logits_kernel, n_rep, n_tp),
        grid=(tiles,),
        out_shape=(
            jax.ShapeDtypeStruct((rows, features), bf16),
            jax.ShapeDtypeStruct((share, columns), f32),
            jax.ShapeDtypeStruct((rows, LANES), f32),
        )
        + tuple(
            jax.ShapeDtypeStruct((share, columns + LANES), jnp.int16) for _ in range(n_tp - 1)
        ),
        in_specs=[whole() for _ in range(3 + len(helds))] + [whole(pltpu.HBM)],
        out_specs=tuple(whole() for _ in range(n_tp + 2)),
        scratch_shapes=[
            pltpu.VMEM((rows, features), bf16),
            pltpu.VMEM((rows, columns), f32),
            pltpu.VMEM((features, rest), f32),
            pltpu.SemaphoreType.DMA((rest // TILE,)),
        ],
        compiler_params=pltpu.CompilerParams(vmem_limit_bytes=14 * MIB),
        cost_estimate=pl.CostEstimate(
            flops=6 * rows * features * columns,
            bytes_accessed=4 * features * columns,
            transcendentals=0,
        ),
        name="partial_logits",
    )(*blocks, gain, *helds, in_hbm(weight))


def decoded(ref, columns):
    share = ref.shape[0]
    tail = ref[:, columns:].astype(jnp.int32).astype(f32)
    part = lax.broadcasted_iota(jnp.int32, (share, LANES), 1) % (LANES // lax.axis_size("tp"))
    unit = jnp.where(part == 0, 16.0, jnp.where(part == 1, 1.0 / 2048.0, 2.0**-26))
    unit = jnp.where(part < 3, unit, 0.0)
    value = ref[:, :columns].astype(jnp.int32).astype(f32)
    return value * jnp.exp2(tail[:, 3:4] - 15.0), tail * unit


def softmax_kernel(n_tp, n_more, own_ref, square_ref, *refs):
    received = refs[: n_tp - 1]
    left_ref, right_ref, scale_ref = refs[n_tp - 1 + n_more : n_tp + 2 + n_more]
    share, columns = own_ref.shape
    group = LANES // n_tp
    lane = lax.broadcasted_iota(jnp.int32, (share, LANES), 1)
    logits, squares = own_ref[...], jnp.zeros((share, LANES), f32)
    for ref in received:
        value, more = decoded(ref, columns)
        logits, squares = logits + value, squares + more
    for j in range(n_tp):
        rows = slice(j * share, (j + 1) * share)
        mine = jnp.where((lane >= j * group) & (lane < (j + 1) * group), squares, 0.0)
        total = square_ref[rows, :] + jnp.sum(mine, axis=-1, keepdims=True)
        scale_ref[rows, :] = lax.rsqrt(total / D + 1e-05)
    tp = lax.axis_index("tp")
    scale = scale_ref[pl.ds(pl.multiple_of(tp * share, share), share), :]
    logits = logits * scale[:, :1]
    top = jnp.max(logits, axis=-1, keepdims=True)
    expo = jnp.exp(logits - top)
    total = jnp.sum(expo, axis=-1, keepdims=True)
    width = right_ref.shape[1]
    place = columns - width
    left_ref[:, :place] = expo[:, :place].astype(bf16)
    right_ref[...] = expo[:, place:].astype(bf16)
    for value in (top, total):
        for _ in range(3):
            high = value.astype(bf16)
            left_ref[:, place : place + 1] = high
            value = value - high.astype(f32)
            place += 1


def held_shapes(helds):
    return tuple(pltpu.VMEM(held.shape, f32) for held in helds)


def run_softmax(own, squares, received, after, helds):
    share, columns = own.shape
    rows = squares.shape[0]
    return pl.pallas_call(
        functools.partial(softmax_kernel, len(received) + 1, len(after) + len(helds)),
        out_shape=(
            jax.ShapeDtypeStruct((share, AGAIN[0] + LANES), bf16),
            jax.ShapeDtypeStruct((share, columns - AGAIN[0]), bf16),
            jax.ShapeDtypeStruct((rows, LANES), f32),
        )
        + held_shapes(helds),
        in_specs=[whole() for _ in range(len(received) + 2)] + [whole(pl.ANY) for _ in after]
        + [whole() for _ in helds],
        out_specs=tuple(whole() for _ in range(3 + len(helds))),
        input_output_aliases={len(received) + len(after) + 2 + i: 3 + i for i in range(len(helds))},
        compiler_params=pltpu.CompilerParams(vmem_limit_bytes=8 * MIB),
        cost_estimate=pl.CostEstimate(flops=65536, bytes_accessed=65536, transcendentals=0),
        name="local_softmax",
    )(own, squares, *received, *after, *helds)


def stats_kernel(n_tp, n_held, *refs):
    stats, out_ref, column_buf = refs[:n_tp], refs[n_tp + n_held], refs[-1]
    share = stats[0].shape[0]
    tp = lax.axis_index("tp")
    lane = lax.broadcasted_iota(jnp.int32, (share, LANES), 1)
    for k, ref in zip((0, *BACK_ORDER), stats):
        parts = ref[:, ref.shape[1] - LANES :].astype(f32)
        top = parts[:, 0:1] + parts[:, 1:2] + parts[:, 2:3]
        total = parts[:, 3:4] + parts[:, 4:5] + parts[:, 5:6]
        place = pl.multiple_of(lax.bitwise_xor(tp, k) * share, share)
        column_buf[pl.ds(place, share), :] = jnp.where(lane == 0, top, total)
    out_ref[...] = column_buf[...].T[:8, :]


def run_stats(lefts, helds):
    rows = len(lefts) * lefts[0].shape[0]
    return pl.pallas_call(
        functools.partial(stats_kernel, len(lefts), len(helds)),
        out_shape=(jax.ShapeDtypeStruct((8, rows), f32),) + held_shapes(helds),
        in_specs=[whole() for _ in range(len(lefts) + len(helds))],
        out_specs=tuple(whole() for _ in range(1 + len(helds))),
        input_output_aliases={len(lefts) + i: 1 + i for i in range(len(helds))},
        scratch_shapes=[pltpu.VMEM((rows, LANES), f32)],
        compiler_params=pltpu.CompilerParams(vmem_limit_bytes=8 * MIB),
        cost_estimate=pl.CostEstimate(flops=65536, bytes_accessed=65536, transcendentals=0),
        name="row_stats",
    )(*lefts, *helds)


def joined(stats):
    top = stats[0][0:1, :]
    for ref in stats[1:]:
        top = jnp.maximum(top, ref[0:1, :])
    total = jnp.zeros_like(top)
    for ref in stats:
        total = total + ref[1:2, :] * jnp.exp(ref[0:1, :] - top)
    return top, total


def join_kernel(first_ref, second_ref, out_ref):
    top, total = joined((first_ref, second_ref))
    row = lax.broadcasted_iota(jnp.int32, out_ref.shape, 0)
    out_ref[...] = jnp.where(row == 0, top, total)


def run_join(first, second):
    return pl.pallas_call(
        join_kernel,
        out_shape=jax.ShapeDtypeStruct(first.shape, f32),
        in_specs=[whole(), whole()],
        out_specs=whole(),
        compiler_params=pltpu.CompilerParams(vmem_limit_bytes=4 * MIB),
        cost_estimate=pl.CostEstimate(flops=4096, bytes_accessed=4096, transcendentals=0),
        name="pair_stats",
    )(first, second)


def turn_kernel(x_ref, gain_ref, out_ref):
    out_ref[...] = (x_ref[...].astype(f32) * gain_ref[...]).T


def run_turn(x, gain):
    rows, features = x.shape
    tile = 1024
    return pl.pallas_call(
        turn_kernel,
        grid=(features // tile,),
        out_shape=jax.ShapeDtypeStruct((features, rows), f32),
        in_specs=[
            pl.BlockSpec((rows, tile), lambda i: (0, i)),
            pl.BlockSpec((1, tile), lambda i: (0, i)),
        ],
        out_specs=pl.BlockSpec((tile, rows), lambda i: (i, 0)),
        compiler_params=pltpu.CompilerParams(vmem_limit_bytes=8 * MIB),
        cost_estimate=pl.CostEstimate(flops=4096, bytes_accessed=4096, transcendentals=0),
        name="turned_rows",
    )(x, gain)


def scale_kernel(
    n_held, first, turned_ref, scale_ref, targets_ref, accepted_ref, weight_ref, *refs
):
    out_ref, target_ref = refs[n_held : n_held + 2]
    rest_ref, sems = refs[-2:]
    copies = column_copies(weight_ref, rest_ref, sems, first)
    for copy in copies:
        copy.start()
    rows = turned_ref.shape[1]
    scale = scale_ref[...].T[:1, :] * learn_rate
    high, low = split2(turned_ref[...] * scale)
    out_ref[:, :rows] = high
    out_ref[:, rows:] = low
    each = targets_ref.shape[1]
    row = lax.broadcasted_iota(jnp.int32, (each, LANES), 0)
    for block in range(rows // each):
        target = jnp.zeros((each, LANES), jnp.int32)
        for i in range(each):
            target = jnp.where(row == i, targets_ref[block, i], target)
        target = jnp.where(row < accepted_ref[block], target, -1)
        target_ref[block * each : (block + 1) * each, :] = target
    for copy in copies:
        copy.wait()


def run_scale(turned, scale, targets, accepted, weight, helds):
    features, rows = turned.shape
    first = sum(held.shape[1] for held in helds)
    rest = weight.shape[1] - first
    return pl.pallas_call(
        functools.partial(scale_kernel, len(helds), first),
        out_shape=(
            jax.ShapeDtypeStruct((features, 2 * rows), bf16),
            jax.ShapeDtypeStruct((rows, LANES), jnp.int32),
        )
        + held_shapes(helds)
        + (pltpu.VMEM((features, rest), f32),),
        in_specs=[
            whole(),
            whole(),
            whole(pltpu.SMEM),
            whole(pltpu.SMEM),
            whole(pltpu.HBM),
        ]
        + [whole() for _ in helds],
        out_specs=tuple(whole() for _ in range(3 + len(helds))),
        input_output_aliases={5 + i: 2 + i for i in range(len(helds))},
        scratch_shapes=[pltpu.SemaphoreType.DMA((rest // 256,))],
        compiler_params=pltpu.CompilerParams(vmem_limit_bytes=8 * MIB),
        cost_estimate=pl.CostEstimate(flops=65536, bytes_accessed=65536, transcendentals=0),
        name="scaled_rows",
    )(turned, scale, targets, accepted, in_hbm(weight), *helds)


def update_kernel(n_tp, n_held, n_kept, first, total_columns, *refs):
    turned_ref, target_ref = refs[:2]
    expo_refs = refs[2 : 2 + n_tp]
    own_stat_ref, *stat_refs = refs[2 + n_tp : 3 + 2 * n_tp]
    out_ref, *held_refs = refs[-4 - n_held - n_kept : -3 - n_kept]
    delta_buf, factor_buf, sems = refs[-3:]
    rep, tp = lax.axis_index("rep"), lax.axis_index("tp")
    share = expo_refs[0].shape[0]
    rows, columns = n_tp * share, delta_buf.shape[1]
    top, total = joined(stat_refs)
    factor = jnp.exp(own_stat_ref[0:1, :] - top) / total
    factor = jnp.broadcast_to(factor, (rows, rows)).T
    trained = jnp.where(target_ref[...] >= 0, 1.0, 0.0)
    factor_buf[...] = factor[:, :LANES] * trained
    label = lax.broadcasted_iota(jnp.int32, (share, columns), 1) + (rep * total_columns + first)
    for k, ref in zip((0, *BACK_ORDER), expo_refs):
        place = pl.multiple_of(lax.bitwise_xor(tp, k) * share, share)
        mine = pl.ds(place, share)
        onehot = jnp.where(label == target_ref[mine, 0:1], 1.0, 0.0)
        delta = ref[:, :columns].astype(f32) * factor_buf[mine, 0:1] - onehot
        delta = delta.astype(bf16)
        delta_buf[mine, :] = delta
        delta_buf[pl.ds(pl.multiple_of(rows + place, share), share), :] = delta

    height = HEIGHT
    steps = turned_ref.shape[0] // height

    def copies_of(step):
        mine = pl.ds(pl.multiple_of(step * height, height), height)
        place, copies = first, []
        for index, ref in enumerate(held_refs):
            target = out_ref.at[mine, pl.ds(place, ref.shape[1])]
            copies.append(pltpu.make_async_copy(ref.at[mine], target, sems.at[index, step]))
            place += ref.shape[1]
        return copies

    def one_step(step, _):
        mine = pl.ds(pl.multiple_of(step * height, height), height)
        grad = jnp.dot(turned_ref[mine, :], delta_buf[...], preferred_element_type=f32)
        place = 0
        for ref in held_refs:
            ref[mine, :] = ref[mine, :] - grad[:, place : place + ref.shape[1]]
            place += ref.shape[1]
        for copy in copies_of(step):
            copy.start()
        return 0

    def one_wait(step, _):
        for copy in copies_of(step):
            copy.wait()
        return 0

    lax.fori_loop(0, steps, one_step, 0)
    lax.fori_loop(0, steps, one_wait, 0)


def run_update(turned, target, expos, stats, helds, kept, first, total_columns, out=None):
    features, pair = turned.shape
    columns = sum(held.shape[1] for held in helds)
    n_tp, n_held = len(expos), len(helds)
    earlier = () if out is None else (out,)
    pieces = (*helds, *kept)
    inputs = (turned, target, *expos, *stats)
    before = len(inputs) + len(earlier)
    aliases = {before + i: 1 + i for i in range(len(pieces))}
    if earlier:
        aliases[len(inputs)] = 0
    new_weight, *pieces = pl.pallas_call(
        functools.partial(update_kernel, n_tp, n_held, len(kept), first, total_columns),
        out_shape=(jax.ShapeDtypeStruct((features, total_columns), f32),) + held_shapes(pieces),
        in_specs=[whole() for _ in inputs]
        + [whole(pltpu.HBM) for _ in earlier]
        + [whole() for _ in pieces],
        out_specs=(whole(pltpu.HBM),) + tuple(whole() for _ in pieces),
        input_output_aliases=aliases,
        scratch_shapes=[
            pltpu.VMEM((pair, columns), bf16),
            pltpu.VMEM((pair // 2, LANES), f32),
            pltpu.SemaphoreType.DMA((n_held, features // HEIGHT)),
        ],
        compiler_params=pltpu.CompilerParams(vmem_limit_bytes=10 * MIB),
        cost_estimate=pl.CostEstimate(
            flops=2 * pair * features * columns,
            bytes_accessed=4 * features * columns,
            transcendentals=0,
        ),
        name="weight_update",
    )(*inputs, *earlier, *pieces)
    return new_weight, pieces[n_held:]


def direct_plan(
    queries,
    cache_keys,
    cache_values,
    page_table,
    lengths,
    history,
    norm_gain,
    draft_weight,
    targets,
    accepted,
):
    n_rep, n_tp = lax.axis_size("rep"), lax.axis_size("tp")
    gain = norm_gain.reshape(1, -1)
    raw, attended, first = run_attention(
        queries[0],
        cache_keys[0, 0],
        cache_values[0, 0],
        page_table[0, 0],
        lengths,
        history[0],
        draft_weight,
        HELD[0],
    )
    first = pltpu.with_memory_space_constraint(first, pltpu.VMEM)
    (second,), loaded = run_load(draft_weight, raw, HELD[0], HELD[1:])
    raws = [raw] + [exchange(raw, "rep", k) for k in range(2, n_rep, 2)]
    block = run_stack(raws, loaded)
    blocks = (block, exchange(block, "rep", 1))
    x, own, squares, *sends = run_logits(
        blocks, gain, (first, second), draft_weight, n_rep, n_tp
    )
    turned = run_turn(x, gain)
    received = [exchange(sends[k - 1], "tp", k) for k in SUM_ORDER]
    helds, loaded = run_load(draft_weight, own, 0, AGAIN)
    left, right, scale, *helds = run_softmax(own, squares, received, (loaded, turned), helds)
    lefts = [left] + [exchange(left, "tp", k) for k in BACK_ORDER]
    scaled, target, *helds = run_scale(turned, scale, targets, accepted, draft_weight, helds)
    stat, *helds = run_stats(lefts, helds)
    pair = run_join(stat, exchange(stat, "rep", 1))
    stats = [stat, pair] + [exchange(pair, "rep", k) for k in range(2, n_rep, 2)]
    helds = [pltpu.with_memory_space_constraint(held, pltpu.VMEM) for held in helds]
    columns = draft_weight.shape[1]
    new_weight, kept = run_update(
        scaled, target, lefts, stats, helds[:1], helds[1:], 0, columns
    )
    kept = [pltpu.with_memory_space_constraint(held, pltpu.VMEM) for held in kept]
    rights = [right] + [exchange(right, "tp", k) for k in BACK_ORDER]
    new_weight, _ = run_update(
        scaled, target, rights, stats, kept, (), AGAIN[0], columns, new_weight
    )
    return (attended[None], new_weight)


def solution(mesh):
    plan = direct_plan if (mesh.shape["rep"], mesh.shape["tp"]) == (8, 4) else general_plan
    return jax.shard_map(
        plan,
        mesh=mesh,
        in_specs=(
            P("rep", None, None),
            P("rep", "tp", None, None, None),
            P("rep", "tp", None, None, None),
            P("rep", "tp", None),
            P("rep"),
            P("rep", None, "tp"),
            P("tp"),
            P("tp", "rep"),
            P(),
            P(),
        ),
        out_specs=(P("rep", None, "tp"), P("tp", "rep")),
        check_vma=False,
    )
```

```python
import functools

import jax
import jax.numpy as jnp
from jax import lax
from jax.experimental import pallas as pl
from jax.experimental.pallas import tpu as pltpu
from jax.sharding import PartitionSpec as P

HQ = 128
KVH = 8
HD = 128
D = 16384

learn_rate = 0.5
LANES = 128
MIB = 1024 * 1024
TILE = 512
SUM_ORDER = (2, 1, 3)
BACK_ORDER = (1, 2, 3)
HEIGHT = 512
HELD = (512, 1024)
AGAIN = (768, 1024)
bf16 = jnp.bfloat16
f32 = jnp.float32


def partner_2(value, axis, distance):
    mask = 2**distance
    pairs = [(source, source ^ mask) for source in range(lax.axis_size(axis))]
    return lax.ppermute(value, axis, pairs)


def merged(value, axis, join):
    pieces = jax.tree.map(lambda part: lax.all_gather(part, axis), value)
    head = jax.tree.map(lambda part: part[0], pieces)
    tail = jax.tree.map(lambda part: part[1:], pieces)
    so_far, _ = lax.scan(lambda so_far, share: (join(so_far, share), None), head, tail)
    return so_far


def attend(query, keys, values, position, length, kv_local, group_heads):
    steps = query.shape[0]
    limit = length - steps + jnp.arange(steps, dtype=jnp.int32)
    valid = (position[None, :] <= limit[:, None])[:, None, None, :]
    grouped = query.astype(f32).reshape(steps, kv_local, group_heads, HD)
    scores = jnp.einsum("skgd,pkd->skgp", grouped, keys.astype(f32)) * HD ** (-0.5)
    top = jnp.max(jnp.where(valid, scores, -1e30), axis=-1)
    expo = jnp.where(valid, jnp.exp(scores - top[..., None]), 0.0)
    total = jnp.sum(expo, axis=-1)
    weighted = jnp.einsum("skgp,pkd->skgd", expo, values.astype(f32))
    return (top, total, weighted)


def join_softmax(first, second):
    top = jnp.maximum(first[0], second[0])
    left = jnp.exp(first[0] - top)
    right = jnp.exp(second[0] - top)
    return (
        top,
        first[1] * left + second[1] * right,
        first[2] * left[..., None] + second[2] * right[..., None],
    )


def join_stats(first, second):
    top = jnp.maximum(first[0], second[0])
    return (top, first[1] * jnp.exp(first[0] - top) + second[1] * jnp.exp(second[0] - top))


def general_plan(
    queries,
    cache_keys,
    cache_values,
    page_table,
    lengths,
    history,
    norm_gain,
    draft_weight,
    targets,
    accepted,
):
    owner = lax.axis_index("tp")
    owners = lax.axis_size("tp")
    kv_local = cache_keys.shape[4] // HD
    sharing = max(1, owners // KVH)
    group_heads = HQ // KVH
    own_heads = HQ // owners
    segment = owner % sharing
    first_head = owner // sharing * kv_local
    table = page_table[0, 0]
    keys = cache_keys[0, 0][table].reshape(-1, kv_local, HD)
    values = cache_values[0, 0][table].reshape(-1, kv_local, HD)
    pages = table.shape[0]
    slots = cache_keys.shape[3]
    position = (
        (jnp.arange(pages, dtype=jnp.int32)[:, None] * sharing + segment) * slots
        + jnp.arange(slots, dtype=jnp.int32)[None, :]
    ).reshape(-1)
    span = kv_local * group_heads * HD
    query = lax.dynamic_slice_in_dim(queries[0], first_head * group_heads * HD, span, 1)
    state = attend(query, keys, values, position, lengths[0], kv_local, group_heads)
    for section in range(sharing.bit_length() - 1):
        partner = partner_2((state[0], state[1], state[2]), "tp", section)
        state = join_softmax(state, partner)
    top, total, weighted = state
    steps = query.shape[0]
    heads = (weighted / total[..., None]).reshape(steps, kv_local * group_heads, HD)
    chosen = lax.dynamic_slice_in_dim(heads, segment * own_heads, own_heads, 1)
    attended = chosen.reshape(1, steps, own_heads * HD).astype(bf16)
    raw = jnp.concatenate([attended[0], history[0]], axis=0)
    rows_each = raw.shape[0]
    wide = raw.astype(f32)
    squares = lax.psum(jnp.sum(wide * wide, axis=-1), "tp")
    row_scale = lax.rsqrt(squares / D + 1e-05)
    scaled_rows = wide * row_scale[:, None] * norm_gain
    gathered = lax.all_gather(scaled_rows, "rep", axis=0, tiled=True)
    partial_value = jnp.dot(
        gathered, draft_weight, precision=lax.Precision.HIGHEST, preferred_element_type=f32
    )
    logits = lax.psum(partial_value, "tp")
    columns = draft_weight.shape[1]
    column_start = lax.axis_index("rep") * columns
    local_top = jnp.max(logits, axis=-1)
    local_total = jnp.sum(jnp.exp(logits - local_top[:, None]), axis=-1)
    top_all, total_all = merged((local_top, local_total), "rep", join_stats)
    probs = jnp.exp(logits - top_all[:, None]) / total_all[:, None]
    labels = column_start + jnp.arange(columns, dtype=jnp.int32)
    onehot = (targets.reshape(-1)[:, None] == labels[None, :]).astype(f32)
    keep = (
        (jnp.arange(rows_each, dtype=jnp.int32)[None, :] < accepted[:, None])
        .reshape(-1)
        .astype(f32)
    )
    delta = (probs - onehot) * keep[:, None]
    grad = jnp.dot(gathered.T, delta, precision=lax.Precision.HIGHEST, preferred_element_type=f32)
    return (attended, draft_weight - learn_rate * grad)


def exchange(value, axis, mask):
    pairs = [(source, source ^ mask) for source in range(lax.axis_size(axis))]
    return lax.ppermute(value, axis, pairs)


def whole(space=pltpu.VMEM):
    return pl.BlockSpec(memory_space=space)


def in_hbm(value):
    return pltpu.with_memory_space_constraint(value, pltpu.HBM)


def attention_kernel(
    kv_local,
    table_ref,
    length_ref,
    queries_ref,
    keys_ref,
    values_ref,
    history_ref,
    weight_ref,
    raw_ref,
    attended_ref,
    held_ref,
    query_buf,
    key_buf,
    value_buf,
    history_buf,
    query_sem,
    key_sem,
    value_sem,
    history_sem,
    weight_sem,
):
    pages, slots = keys_ref.shape[0], keys_ref.shape[1]
    steps = query_buf.shape[0]
    group = HQ // KVH
    span = query_buf.shape[1]
    start = pl.multiple_of(lax.axis_index("tp") * span, span)
    weight_copies = column_copies(weight_ref, held_ref, weight_sem, 0)
    for copy in weight_copies:
        copy.start()
    query_copy = pltpu.make_async_copy(queries_ref.at[:, pl.ds(start, span)], query_buf, query_sem)
    query_copy.start()
    key_copies, value_copies = [], []
    for source, target, sems, copies in (
        (keys_ref, key_buf, key_sem, key_copies),
        (values_ref, value_buf, value_sem, value_copies),
    ):
        for page in range(pages):
            copy = pltpu.make_async_copy(
                source.at[table_ref[page]], target.at[pl.ds(page * slots, slots)], sems.at[page]
            )
            copy.start()
            copies.append(copy)
    history_copy = pltpu.make_async_copy(history_ref, history_buf, history_sem)
    history_copy.start()
    query_copy.wait()
    queries = query_buf[...].astype(f32)
    stacked = []
    for head in range(kv_local):
        parts = [
            queries[:, (head * group + g) * HD : (head * group + g + 1) * HD] for g in range(group)
        ]
        stacked.append(jnp.concatenate(parts, axis=0).astype(bf16))
    for copy in key_copies:
        copy.wait()
    shape = (group * steps, pages * slots)
    step = lax.broadcasted_iota(jnp.int32, shape, 0) % steps
    position = lax.broadcasted_iota(jnp.int32, shape, 1)
    valid = position <= length_ref[0] - steps + step
    expos, totals = [], []
    for head in range(kv_local):
        scores = lax.dot_general(
            stacked[head],
            key_buf[:, head * HD : (head + 1) * HD],
            (((1,), (1,)), ((), ())),
            preferred_element_type=f32,
        ) * (HD ** (-0.5))
        top = jnp.max(jnp.where(valid, scores, -1e30), axis=-1, keepdims=True)
        expo = jnp.where(valid, jnp.exp(scores - top), 0.0)
        totals.append(jnp.sum(expo, axis=-1, keepdims=True))
        expos.append(jnp.concatenate(split2(expo), axis=0))
    for copy in value_copies:
        copy.wait()
    history_copy.wait()
    for head in range(kv_local):
        both = jnp.dot(
            expos[head],
            value_buf[:, head * HD : (head + 1) * HD],
            preferred_element_type=f32,
        )
        half = group * steps
        out = (both[:half] + both[half:]) / totals[head]
        for g in range(group):
            columns = slice((head * group + g) * HD, (head * group + g + 1) * HD)
            piece = out[g * steps : (g + 1) * steps]
            earlier = history_buf[:, columns].astype(f32)
            raw_ref[:, columns] = jnp.concatenate([piece, earlier], axis=0).astype(bf16)
            attended_ref[:, columns] = piece.astype(bf16)
    for copy in weight_copies:
        copy.wait()


def run_attention(queries, keys, values, table, length, history, weight, held):
    pages, slots, width = keys.shape
    kv_local = width // HD
    steps = queries.shape[0]
    span = kv_local * (HQ // KVH) * HD
    rows = steps + history.shape[0]
    return pl.pallas_call(
        functools.partial(attention_kernel, kv_local),
        out_shape=(
            jax.ShapeDtypeStruct((rows, span), bf16),
            jax.ShapeDtypeStruct((steps, span), bf16),
            pltpu.VMEM((weight.shape[0], held), f32),
        ),
        in_specs=[
            whole(pltpu.SMEM),
            whole(pltpu.SMEM),
            whole(pltpu.HBM),
            whole(pltpu.HBM),
            whole(pltpu.HBM),
            whole(pltpu.HBM),
            whole(pltpu.HBM),
        ],
        out_specs=(whole(), whole(), whole()),
        scratch_shapes=[
            pltpu.VMEM((steps, span), bf16),
            pltpu.VMEM((pages * slots, width), bf16),
            pltpu.VMEM((pages * slots, width), bf16),
            pltpu.VMEM(history.shape, bf16),
            pltpu.SemaphoreType.DMA,
            pltpu.SemaphoreType.DMA((pages,)),
            pltpu.SemaphoreType.DMA((pages,)),
            pltpu.SemaphoreType.DMA,
            pltpu.SemaphoreType.DMA((held // 256,)),
        ],
        compiler_params=pltpu.CompilerParams(vmem_limit_bytes=12 * MIB),
        cost_estimate=pl.CostEstimate(
            flops=4 * 64 * 1024 * 256, bytes_accessed=12 * MIB, transcendentals=131072
        ),
        name="attention",
    )(in_hbm(table), length, *(in_hbm(part) for part in (queries, keys, values, history, weight)))


def column_copies(source, target, sems, first, width=256):
    return [
        pltpu.make_async_copy(
            source.at[:, pl.ds(first + place, width)],
            target.at[:, pl.ds(place, width)],
            sems.at[index],
        )
        for index, place in enumerate(range(0, target.shape[1], width))
    ]


def load_kernel(first, count, weight_ref, token_ref, *refs):
    held_refs, done_ref, sems = refs[:count], refs[count], refs[count + 1]
    done_ref[...] = jnp.zeros(done_ref.shape, f32)
    copies = []
    for ref in held_refs:
        tiles = len(copies)
        copies += column_copies(weight_ref, ref, sems.at[pl.ds(tiles, ref.shape[1] // 256)], first)
        first += ref.shape[1]
    for copy in copies:
        copy.start()
    for copy in copies:
        copy.wait()


def run_load(weight, token, first, widths):
    rows = weight.shape[0]
    columns = sum(widths)
    *helds, done = pl.pallas_call(
        functools.partial(load_kernel, first, len(widths)),
        out_shape=tuple(pltpu.VMEM((rows, width), f32) for width in widths)
        + (jax.ShapeDtypeStruct((8, LANES), f32),),
        in_specs=[whole(pltpu.HBM), whole(pl.ANY)],
        out_specs=tuple(whole() for _ in range(len(widths) + 1)),
        scratch_shapes=[pltpu.SemaphoreType.DMA((columns // 256,))],
        compiler_params=pltpu.CompilerParams(vmem_limit_bytes=8 * MIB),
        cost_estimate=pl.CostEstimate(
            flops=0, bytes_accessed=4 * rows * columns, transcendentals=0
        ),
        name="load_weight",
    )(in_hbm(weight), token)
    return [pltpu.with_memory_space_constraint(held, pltpu.VMEM) for held in helds], done


def split2(value):
    high = value.astype(bf16)
    return high, (value - high.astype(f32)).astype(bf16)


def stack_kernel(*refs):
    each = refs[0].shape[0]
    for k, ref in enumerate(refs[:-2]):
        refs[-1][k * each : (k + 1) * each, :] = ref[...]


def run_stack(parts, after):
    each, features = parts[0].shape
    return pl.pallas_call(
        stack_kernel,
        out_shape=jax.ShapeDtypeStruct((len(parts) * each, features), bf16),
        in_specs=[whole() for _ in parts] + [whole(pl.ANY)],
        out_specs=whole(),
        compiler_params=pltpu.CompilerParams(vmem_limit_bytes=4 * MIB),
        cost_estimate=pl.CostEstimate(flops=4096, bytes_accessed=4096, transcendentals=0),
        name="stacked_rows",
    )(*parts, after)


def power_above(value):
    exponent = jnp.full(value.shape, -96.0, f32)
    for step in (128.0, 64.0, 32.0, 16.0, 8.0, 4.0, 2.0, 1.0):
        exponent = jnp.where(value > jnp.exp2(exponent + (step - 1.0)), exponent + step, exponent)
    return exponent


def logits_kernel(n_rep, n_tp, *refs):
    block_refs = refs[:2]
    gain_ref, *held_refs, weight_ref = refs[2:6]
    x_ref, own_ref, square_ref = refs[6:9]
    send_refs = refs[9 : 8 + n_tp]
    scaled_buf, partial_buf, rest_buf, rest_sem = refs[8 + n_tp :]
    tile = pl.program_id(0)
    rep, tp = lax.axis_index("rep"), lax.axis_index("tp")
    rows = x_ref.shape[0]
    each = rows // n_rep
    share = rows // n_tp
    width = partial_buf.shape[1] // pl.num_programs(0)
    held_columns = sum(ref.shape[1] for ref in held_refs)
    copies = column_copies(weight_ref, rest_buf, rest_sem, held_columns, width)

    @pl.when(tile == 0)
    def _():
        for copy in copies:
            copy.start()
        for k in range(n_rep):
            block = block_refs[k % 2][k // 2 * each : (k // 2 + 1) * each, :]
            place = pl.multiple_of(lax.bitwise_xor(rep, k) * each, each)
            x_ref[pl.ds(place, each), :] = block
            value = block.astype(f32)
            squares = jnp.sum(value * value, axis=-1, keepdims=True)
            square_ref[pl.ds(place, each), :] = jnp.broadcast_to(squares, (each, LANES))
            scaled_buf[pl.ds(place, each), :] = (value * gain_ref[...]).astype(bf16)

    columns = pl.ds(pl.multiple_of(tile * width, width), width)

    def multiply(weight):
        partial_buf[:, columns] = jnp.dot(
            scaled_buf[...], weight.astype(bf16), preferred_element_type=f32
        )

    first = 0
    for ref in held_refs:
        for index in range(ref.shape[1] // width):

            @pl.when(tile == first + index)
            def _():
                multiply(ref[:, index * width : (index + 1) * width])

        first += ref.shape[1] // width
    for index, copy in enumerate(copies):

        @pl.when(tile == first + index)
        def _():
            copy.wait()
            multiply(rest_buf[:, index * width : (index + 1) * width])

    @pl.when(tile == pl.num_programs(0) - 1)
    def _():
        own_ref[...] = partial_buf[pl.ds(pl.multiple_of(tp * share, share), share), :]
        full = partial_buf.shape[1]
        lane = lax.broadcasted_iota(jnp.int32, (share, LANES), 1)
        squares = jnp.zeros((share, LANES), f32)
        group = LANES // n_tp
        for j in range(n_tp):
            mine = (lane >= j * group) & (lane < (j + 1) * group)
            squares = jnp.where(mine, square_ref[j * share : (j + 1) * share, :], squares)
        first = jnp.floor(squares / 16.0)
        second = jnp.floor((squares - first * 16.0) * 2048.0)
        third = jnp.floor((squares - first * 16.0 - second / 2048.0) * 2.0**26)
        part = lane % group
        extra = jnp.where(part == 0, first, jnp.where(part == 1, second, third))
        for k in range(1, n_tp):
            place = pl.multiple_of(lax.bitwise_xor(tp, k) * share, share)
            value = partial_buf[pl.ds(place, share), :]
            exponent = power_above(jnp.max(jnp.abs(value), axis=-1, keepdims=True))
            coded = jnp.floor(value * jnp.exp2(15.0 - exponent) + 0.5)
            coded = jnp.clip(coded, -32768.0, 32767.0)
            send_refs[k - 1][:, :full] = coded.astype(jnp.int32).astype(jnp.int16)
            tail = jnp.where(part == 3, exponent, extra)
            send_refs[k - 1][:, full:] = tail.astype(jnp.int32).astype(jnp.int16)


def run_logits(blocks, gain, helds, weight, n_rep, n_tp):
    rows, features = 2 * blocks[0].shape[0], blocks[0].shape[1]
    columns = weight.shape[1]
    share = rows // n_tp
    tiles = columns // TILE
    rest = columns - sum(held.shape[1] for held in helds)
    return pl.pallas_call(
        functools.partial(logits_kernel, n_rep, n_tp),
        grid=(tiles,),
        out_shape=(
            jax.ShapeDtypeStruct((rows, features), bf16),
            jax.ShapeDtypeStruct((share, columns), f32),
            jax.ShapeDtypeStruct((rows, LANES), f32),
        )
        + tuple(
            jax.ShapeDtypeStruct((share, columns + LANES), jnp.int16) for _ in range(n_tp - 1)
        ),
        in_specs=[whole() for _ in range(3 + len(helds))] + [whole(pltpu.HBM)],
        out_specs=tuple(whole() for _ in range(n_tp + 2)),
        scratch_shapes=[
            pltpu.VMEM((rows, features), bf16),
            pltpu.VMEM((rows, columns), f32),
            pltpu.VMEM((features, rest), f32),
            pltpu.SemaphoreType.DMA((rest // TILE,)),
        ],
        compiler_params=pltpu.CompilerParams(vmem_limit_bytes=14 * MIB),
        cost_estimate=pl.CostEstimate(
            flops=6 * rows * features * columns,
            bytes_accessed=4 * features * columns,
            transcendentals=0,
        ),
        name="partial_logits",
    )(*blocks, gain, *helds, in_hbm(weight))


def decoded(ref, columns):
    share = ref.shape[0]
    tail = ref[:, columns:].astype(jnp.int32).astype(f32)
    part = lax.broadcasted_iota(jnp.int32, (share, LANES), 1) % (LANES // lax.axis_size("tp"))
    unit = jnp.where(part == 0, 16.0, jnp.where(part == 1, 1.0 / 2048.0, 2.0**-26))
    unit = jnp.where(part < 3, unit, 0.0)
    value = ref[:, :columns].astype(jnp.int32).astype(f32)
    return value * jnp.exp2(tail[:, 3:4] - 15.0), tail * unit


def softmax_kernel(n_tp, n_more, own_ref, square_ref, *refs):
    received = refs[: n_tp - 1]
    left_ref, right_ref, scale_ref = refs[n_tp - 1 + n_more : n_tp + 2 + n_more]
    share, columns = own_ref.shape
    group = LANES // n_tp
    lane = lax.broadcasted_iota(jnp.int32, (share, LANES), 1)
    logits, squares = own_ref[...], jnp.zeros((share, LANES), f32)
    for ref in received:
        value, more = decoded(ref, columns)
        logits, squares = logits + value, squares + more
    for j in range(n_tp):
        rows = slice(j * share, (j + 1) * share)
        mine = jnp.where((lane >= j * group) & (lane < (j + 1) * group), squares, 0.0)
        total = square_ref[rows, :] + jnp.sum(mine, axis=-1, keepdims=True)
        scale_ref[rows, :] = lax.rsqrt(total / D + 1e-05)
    tp = lax.axis_index("tp")
    scale = scale_ref[pl.ds(pl.multiple_of(tp * share, share), share), :]
    logits = logits * scale[:, :1]
    top = jnp.max(logits, axis=-1, keepdims=True)
    expo = jnp.exp(logits - top)
    total = jnp.sum(expo, axis=-1, keepdims=True)
    width = right_ref.shape[1]
    place = columns - width
    left_ref[:, :place] = expo[:, :place].astype(bf16)
    right_ref[...] = expo[:, place:].astype(bf16)
    for value in (top, total):
        for _ in range(3):
            high = value.astype(bf16)
            left_ref[:, place : place + 1] = high
            value = value - high.astype(f32)
            place += 1


def held_shapes(helds):
    return tuple(pltpu.VMEM(held.shape, f32) for held in helds)


def run_softmax(own, squares, received, after, helds):
    share, columns = own.shape
    rows = squares.shape[0]
    return pl.pallas_call(
        functools.partial(softmax_kernel, len(received) + 1, len(after) + len(helds)),
        out_shape=(
            jax.ShapeDtypeStruct((share, AGAIN[0] + LANES), bf16),
            jax.ShapeDtypeStruct((share, columns - AGAIN[0]), bf16),
            jax.ShapeDtypeStruct((rows, LANES), f32),
        )
        + held_shapes(helds),
        in_specs=[whole() for _ in range(len(received) + 2)] + [whole(pl.ANY) for _ in after]
        + [whole() for _ in helds],
        out_specs=tuple(whole() for _ in range(3 + len(helds))),
        input_output_aliases={len(received) + len(after) + 2 + i: 3 + i for i in range(len(helds))},
        compiler_params=pltpu.CompilerParams(vmem_limit_bytes=8 * MIB),
        cost_estimate=pl.CostEstimate(flops=65536, bytes_accessed=65536, transcendentals=0),
        name="local_softmax",
    )(own, squares, *received, *after, *helds)


def stats_kernel(n_tp, n_held, *refs):
    stats, out_ref, column_buf = refs[:n_tp], refs[n_tp + n_held], refs[-1]
    share = stats[0].shape[0]
    tp = lax.axis_index("tp")
    lane = lax.broadcasted_iota(jnp.int32, (share, LANES), 1)
    for k, ref in zip((0, *BACK_ORDER), stats):
        parts = ref[:, ref.shape[1] - LANES :].astype(f32)
        top = parts[:, 0:1] + parts[:, 1:2] + parts[:, 2:3]
        total = parts[:, 3:4] + parts[:, 4:5] + parts[:, 5:6]
        place = pl.multiple_of(lax.bitwise_xor(tp, k) * share, share)
        column_buf[pl.ds(place, share), :] = jnp.where(lane == 0, top, total)
    out_ref[...] = column_buf[...].T[:8, :]


def run_stats(lefts, helds):
    rows = len(lefts) * lefts[0].shape[0]
    return pl.pallas_call(
        functools.partial(stats_kernel, len(lefts), len(helds)),
        out_shape=(jax.ShapeDtypeStruct((8, rows), f32),) + held_shapes(helds),
        in_specs=[whole() for _ in range(len(lefts) + len(helds))],
        out_specs=tuple(whole() for _ in range(1 + len(helds))),
        input_output_aliases={len(lefts) + i: 1 + i for i in range(len(helds))},
        scratch_shapes=[pltpu.VMEM((rows, LANES), f32)],
        compiler_params=pltpu.CompilerParams(vmem_limit_bytes=8 * MIB),
        cost_estimate=pl.CostEstimate(flops=65536, bytes_accessed=65536, transcendentals=0),
        name="row_stats",
    )(*lefts, *helds)


def joined(stats):
    top = stats[0][0:1, :]
    for ref in stats[1:]:
        top = jnp.maximum(top, ref[0:1, :])
    total = jnp.zeros_like(top)
    for ref in stats:
        total = total + ref[1:2, :] * jnp.exp(ref[0:1, :] - top)
    return top, total


def join_kernel(first_ref, second_ref, out_ref):
    top, total = joined((first_ref, second_ref))
    row = lax.broadcasted_iota(jnp.int32, out_ref.shape, 0)
    out_ref[...] = jnp.where(row == 0, top, total)


def run_join(first, second):
    return pl.pallas_call(
        join_kernel,
        out_shape=jax.ShapeDtypeStruct(first.shape, f32),
        in_specs=[whole(), whole()],
        out_specs=whole(),
        compiler_params=pltpu.CompilerParams(vmem_limit_bytes=4 * MIB),
        cost_estimate=pl.CostEstimate(flops=4096, bytes_accessed=4096, transcendentals=0),
        name="pair_stats",
    )(first, second)


def turn_kernel(x_ref, gain_ref, out_ref):
    out_ref[...] = (x_ref[...].astype(f32) * gain_ref[...]).T


def run_turn(x, gain):
    rows, features = x.shape
    tile = 1024
    return pl.pallas_call(
        turn_kernel,
        grid=(features // tile,),
        out_shape=jax.ShapeDtypeStruct((features, rows), f32),
        in_specs=[
            pl.BlockSpec((rows, tile), lambda i: (0, i)),
            pl.BlockSpec((1, tile), lambda i: (0, i)),
        ],
        out_specs=pl.BlockSpec((tile, rows), lambda i: (i, 0)),
        compiler_params=pltpu.CompilerParams(vmem_limit_bytes=8 * MIB),
        cost_estimate=pl.CostEstimate(flops=4096, bytes_accessed=4096, transcendentals=0),
        name="turned_rows",
    )(x, gain)


def scale_kernel(
    n_held, first, turned_ref, scale_ref, targets_ref, accepted_ref, weight_ref, *refs
):
    out_ref, target_ref = refs[n_held : n_held + 2]
    rest_ref, sems = refs[-2:]
    copies = column_copies(weight_ref, rest_ref, sems, first)
    for copy in copies:
        copy.start()
    rows = turned_ref.shape[1]
    scale = scale_ref[...].T[:1, :] * learn_rate
    high, low = split2(turned_ref[...] * scale)
    out_ref[:, :rows] = high
    out_ref[:, rows:] = low
    each = targets_ref.shape[1]
    row = lax.broadcasted_iota(jnp.int32, (each, LANES), 0)
    for block in range(rows // each):
        target = jnp.zeros((each, LANES), jnp.int32)
        for i in range(each):
            target = jnp.where(row == i, targets_ref[block, i], target)
        target = jnp.where(row < accepted_ref[block], target, -1)
        target_ref[block * each : (block + 1) * each, :] = target
    for copy in copies:
        copy.wait()


def run_scale(turned, scale, targets, accepted, weight, helds):
    features, rows = turned.shape
    first = sum(held.shape[1] for held in helds)
    rest = weight.shape[1] - first
    return pl.pallas_call(
        functools.partial(scale_kernel, len(helds), first),
        out_shape=(
            jax.ShapeDtypeStruct((features, 2 * rows), bf16),
            jax.ShapeDtypeStruct((rows, LANES), jnp.int32),
        )
        + held_shapes(helds)
        + (pltpu.VMEM((features, rest), f32),),
        in_specs=[
            whole(),
            whole(),
            whole(pltpu.SMEM),
            whole(pltpu.SMEM),
            whole(pltpu.HBM),
        ]
        + [whole() for _ in helds],
        out_specs=tuple(whole() for _ in range(3 + len(helds))),
        input_output_aliases={5 + i: 2 + i for i in range(len(helds))},
        scratch_shapes=[pltpu.SemaphoreType.DMA((rest // 256,))],
        compiler_params=pltpu.CompilerParams(vmem_limit_bytes=8 * MIB),
        cost_estimate=pl.CostEstimate(flops=65536, bytes_accessed=65536, transcendentals=0),
        name="scaled_rows",
    )(turned, scale, targets, accepted, in_hbm(weight), *helds)


def update_kernel(n_tp, n_held, n_kept, first, total_columns, *refs):
    turned_ref, target_ref = refs[:2]
    expo_refs = refs[2 : 2 + n_tp]
    own_stat_ref, *stat_refs = refs[2 + n_tp : 3 + 2 * n_tp]
    out_ref, *held_refs = refs[-4 - n_held - n_kept : -3 - n_kept]
    delta_buf, factor_buf, sems = refs[-3:]
    rep, tp = lax.axis_index("rep"), lax.axis_index("tp")
    share = expo_refs[0].shape[0]
    rows, columns = n_tp * share, delta_buf.shape[1]
    top, total = joined(stat_refs)
    factor = jnp.exp(own_stat_ref[0:1, :] - top) / total
    factor = jnp.broadcast_to(factor, (rows, rows)).T
    trained = jnp.where(target_ref[...] >= 0, 1.0, 0.0)
    factor_buf[...] = factor[:, :LANES] * trained
    label = lax.broadcasted_iota(jnp.int32, (share, columns), 1) + (rep * total_columns + first)
    for k, ref in zip((0, *BACK_ORDER), expo_refs):
        place = pl.multiple_of(lax.bitwise_xor(tp, k) * share, share)
        mine = pl.ds(place, share)
        onehot = jnp.where(label == target_ref[mine, 0:1], 1.0, 0.0)
        delta = ref[:, :columns].astype(f32) * factor_buf[mine, 0:1] - onehot
        delta = delta.astype(bf16)
        delta_buf[mine, :] = delta
        delta_buf[pl.ds(pl.multiple_of(rows + place, share), share), :] = delta

    height = HEIGHT
    steps = turned_ref.shape[0] // height

    def copies_of(step):
        mine = pl.ds(pl.multiple_of(step * height, height), height)
        place, copies = first, []
        for index, ref in enumerate(held_refs):
            target = out_ref.at[mine, pl.ds(place, ref.shape[1])]
            copies.append(pltpu.make_async_copy(ref.at[mine], target, sems.at[index, step]))
            place += ref.shape[1]
        return copies

    def one_step(step, _):
        mine = pl.ds(pl.multiple_of(step * height, height), height)
        grad = jnp.dot(turned_ref[mine, :], delta_buf[...], preferred_element_type=f32)
        place = 0
        for ref in held_refs:
            ref[mine, :] = ref[mine, :] - grad[:, place : place + ref.shape[1]]
            place += ref.shape[1]
        for copy in copies_of(step):
            copy.start()
        return 0

    def one_wait(step, _):
        for copy in copies_of(step):
            copy.wait()
        return 0

    lax.fori_loop(0, steps, one_step, 0)
    lax.fori_loop(0, steps, one_wait, 0)


def run_update(turned, target, expos, stats, helds, kept, first, total_columns, out=None):
    features, pair = turned.shape
    columns = sum(held.shape[1] for held in helds)
    n_tp, n_held = len(expos), len(helds)
    earlier = () if out is None else (out,)
    pieces = (*helds, *kept)
    inputs = (turned, target, *expos, *stats)
    before = len(inputs) + len(earlier)
    aliases = {before + i: 1 + i for i in range(len(pieces))}
    if earlier:
        aliases[len(inputs)] = 0
    new_weight, *pieces = pl.pallas_call(
        functools.partial(update_kernel, n_tp, n_held, len(kept), first, total_columns),
        out_shape=(jax.ShapeDtypeStruct((features, total_columns), f32),) + held_shapes(pieces),
        in_specs=[whole() for _ in inputs]
        + [whole(pltpu.HBM) for _ in earlier]
        + [whole() for _ in pieces],
        out_specs=(whole(pltpu.HBM),) + tuple(whole() for _ in pieces),
        input_output_aliases=aliases,
        scratch_shapes=[
            pltpu.VMEM((pair, columns), bf16),
            pltpu.VMEM((pair // 2, LANES), f32),
            pltpu.SemaphoreType.DMA((n_held, features // HEIGHT)),
        ],
        compiler_params=pltpu.CompilerParams(vmem_limit_bytes=10 * MIB),
        cost_estimate=pl.CostEstimate(
            flops=2 * pair * features * columns,
            bytes_accessed=4 * features * columns,
            transcendentals=0,
        ),
        name="weight_update",
    )(*inputs, *earlier, *pieces)
    return new_weight, pieces[n_held:]


def direct_plan(
    queries,
    cache_keys,
    cache_values,
    page_table,
    lengths,
    history,
    norm_gain,
    draft_weight,
    targets,
    accepted,
):
    n_rep, n_tp = lax.axis_size("rep"), lax.axis_size("tp")
    gain = norm_gain.reshape(1, -1)
    raw, attended, first = run_attention(
        queries[0],
        cache_keys[0, 0],
        cache_values[0, 0],
        page_table[0, 0],
        lengths,
        history[0],
        draft_weight,
        HELD[0],
    )
    first = pltpu.with_memory_space_constraint(first, pltpu.VMEM)
    (second,), loaded = run_load(draft_weight, raw, HELD[0], HELD[1:])
    raws = [raw] + [exchange(raw, "rep", k) for k in range(2, n_rep, 2)]
    block = run_stack(raws, loaded)
    blocks = (block, exchange(block, "rep", 1))
    x, own, squares, *sends = run_logits(
        blocks, gain, (first, second), draft_weight, n_rep, n_tp
    )
    turned = run_turn(x, gain)
    received = [exchange(sends[k - 1], "tp", k) for k in SUM_ORDER]
    helds, loaded = run_load(draft_weight, own, 0, AGAIN)
    left, right, scale, *helds = run_softmax(own, squares, received, (loaded,), helds)
    lefts = [left] + [exchange(left, "tp", k) for k in BACK_ORDER]
    scaled, target, *helds = run_scale(turned, scale, targets, accepted, draft_weight, helds)
    stat, *helds = run_stats(lefts, helds)
    pair = run_join(stat, exchange(stat, "rep", 1))
    stats = [stat, pair] + [exchange(pair, "rep", k) for k in range(2, n_rep, 2)]
    helds = [pltpu.with_memory_space_constraint(held, pltpu.VMEM) for held in helds]
    columns = draft_weight.shape[1]
    new_weight, kept = run_update(
        scaled, target, lefts, stats, helds[:1], helds[1:], 0, columns
    )
    kept = [pltpu.with_memory_space_constraint(held, pltpu.VMEM) for held in kept]
    rights = [right] + [exchange(right, "tp", k) for k in BACK_ORDER]
    new_weight, _ = run_update(
        scaled, target, rights, stats, kept, (), AGAIN[0], columns, new_weight
    )
    return (attended[None], new_weight)


def solution(mesh):
    plan = direct_plan if (mesh.shape["rep"], mesh.shape["tp"]) == (8, 4) else general_plan
    return jax.shard_map(
        plan,
        mesh=mesh,
        in_specs=(
            P("rep", None, None),
            P("rep", "tp", None, None, None),
            P("rep", "tp", None, None, None),
            P("rep", "tp", None),
            P("rep"),
            P("rep", None, "tp"),
            P("tp"),
            P("tp", "rep"),
            P(),
            P(),
        ),
        out_specs=(P("rep", None, "tp"), P("tp", "rep")),
        check_vma=False,
    )
```
